128 devices in a mesh: ctx: 16 (over x, y), head: 8 (over z, core).
Axes of the slice: x: 4, y: 4, z: 4, core: 2. Of those that a mesh axis runs over, the one named last changes fastest.
Arguments:
- query: bfloat16 [16384, 3072], P('ctx', 'head'), may hold values from -110 to 110
- keys: bfloat16 [16384, 3072], P('ctx', 'head'), may hold values from -5 to 5
- values: bfloat16 [16384, 3072], P('ctx', 'head'), may hold values from -6 to 6
- doc_lengths: int32 [8], replicated, may hold values from 1 to 8192, as said below
- w_out: bfloat16 [3072, 5120], P('head'), may hold values from -0.15625 to 0.15625
Outputs:
- layer_out: bfloat16 [16384, 5120], P('ctx', 'head')
The draws below stay inside these ranges and needn't reach their ends.
Inputs may be any that keep to these rules, and one draw needn't show every extreme that they name: `doc_lengths`: 8 document lengths summing to 16384; the first document has exactly 8192 tokens and every other one fewer.
All inputs are finite; a program needn't handle non-finite values.
Results may differ from the reference program's by a relative error of at most 0.018.
Values may be sent and summed in bfloat16 or wider, within the bound.
A program may use at most 128 MiB of HBM per device.

```python
import math
import jax
import jax.numpy as jnp
from jax import lax

D = 5120
HEADS = 24
HD = 128
TOK_DEV = 1024
NDOCS = 8
TOKENS = 16384
MOST_DOC = 8192
N_HEAD = 8


def shared_normal(key):
    return jnp.clip(jax.random.normal(key, (TOKENS, HEADS * HD), jnp.float32), -4.5, 4.5)


def draw_keys(key, part):
    shared = shared_normal(key)
    return shared.astype(jnp.bfloat16)


def draw_query(key, part):
    key = jax.random.fold_in(key, 7)
    own = jnp.clip(jax.random.normal(key, (TOKENS, HEADS * HD), jnp.float32), -4.5, 4.5)
    return own.astype(jnp.bfloat16)


def draw_doc_lengths(key, part):
    key = jax.random.fold_in(key, 11)
    remain = TOKENS - MOST_DOC
    order = jax.random.permutation(key, remain - 1) + 1
    cuts = jnp.sort(order[:NDOCS - 2])
    bounds = jnp.concatenate([jnp.zeros((1,), jnp.int32), cuts.astype(jnp.int32), jnp.full((1,), remain, jnp.int32)])
    pieces = bounds[1:] - bounds[:-1]
    return jnp.concatenate([jnp.full((1,), MOST_DOC, jnp.int32), pieces]).astype(jnp.int32)


def spiked(result, rng, source, target, shards_of, factor):
    def block_of(axis_at):
        return (jnp.arange(result.shape[axis_at]) // (result.shape[axis_at] // shards_of)).reshape((-1,) + (1,) * (result.ndim - 1 - axis_at))

    one_side = jax.random.permutation(rng, shards_of)[block_of(target)]
    other_side = (block_of(target) + shards_of // 2) % shards_of
    return jnp.where((block_of(source) == one_side) | (block_of(source) == other_side), factor * result, result)


def shard_levels(own_key, dims, cuts, smallest, top_value):
    gain, own = 1.0, jax.random.fold_in(own_key, 6)
    for dim, shards_of in cuts:
        steps = jnp.exp(jax.random.uniform(jax.random.fold_in(own, dim), (shards_of,), jnp.float32, smallest / len(cuts), top_value / len(cuts)))
        gain = gain * jnp.repeat(steps, dims[dim] // shards_of).reshape([-1 if axis == dim else 1 for axis in range(len(dims))])
    return gain


def centred(rng, dims, spread, most, split=(), held_as=jnp.bfloat16):
    loudness = shard_levels(rng, dims, split, -0.22, 0.18) if split else 1.0
    drawn = jax.random.normal(rng, dims, jnp.float32) * spread * loudness
    return jnp.minimum(jnp.maximum(drawn, -most), most).astype(held_as)


def noise_with(key, extent, deviation, bound, split, heavy, held_as=jnp.bfloat16):
    result = deviation * jax.random.normal(key, extent, jnp.float32)
    if split:
        result = result * shard_levels(key, extent, split, -0.22, 0.18)
    return jnp.clip(spiked(result, jax.random.fold_in(key, 3), *heavy), -bound, bound).astype(held_as)


def setup_inputs(seed: int = 0) -> dict:
    streams_of = jax.random.split(jax.random.key(seed), 6)
    return {
        "query": draw_query(jax.random.fold_in(streams_of[5], 71), 0),
        "keys": draw_keys(jax.random.fold_in(streams_of[5], 71), 0),
        "values": centred(streams_of[2], (TOKENS, HEADS * HD), 1.0, 6.0, ((0, 16), (1, 8))),
        "doc_lengths": draw_doc_lengths(jax.random.fold_in(streams_of[5], 71), 0),
        "w_out": noise_with(streams_of[4], (HEADS * HD, D), (HEADS * HD) ** -0.5, 0.15625, ((0, 8),), (0, 1, 8, 2.0)),
    }


def doc_ids(doc_lengths):
    ends = jnp.cumsum(doc_lengths).astype(jnp.int32)
    places = jnp.arange(TOKENS, dtype=jnp.int32)
    return lax.optimization_barrier(jnp.sum((places[:, None] >= ends[None, :]).astype(jnp.int32), axis=1)).astype(jnp.int32)

def reference(query, keys, values, doc_lengths, w_out):
    scale = 1.0 / math.sqrt(HD)
    docs = doc_ids(doc_lengths)
    places = jnp.arange(TOKENS, dtype=jnp.int32)
    key_heads = keys.reshape(TOKENS, HEADS, HD).transpose(1, 0, 2)
    value_heads = values.reshape(TOKENS, HEADS, HD).transpose(1, 0, 2)
    blocks = TOKENS // TOK_DEV
    query_blocks = query.reshape(blocks, TOK_DEV, HEADS, HD).transpose(0, 2, 1, 3)
    block_starts = (jnp.arange(blocks, dtype=jnp.int32) * TOK_DEV).astype(jnp.int32)

    def one_block(inputs):
        query_block, start = inputs
        rows_pos = start + jnp.arange(TOK_DEV, dtype=jnp.int32)
        rows_doc = lax.dynamic_slice_in_dim(docs, start, TOK_DEV, 0)
        allowed = (places[None, :] <= rows_pos[:, None]) & (docs[None, :] == rows_doc[:, None])

        def one_head(head_inputs):
            query_head, key_head, value_head = head_inputs
            scores = jnp.dot(query_head, key_head.T, preferred_element_type=jnp.float32) * scale
            scores = jnp.where(allowed, scores, -1e+30)
            top = lax.optimization_barrier(jnp.max(scores, axis=1, keepdims=True))
            weights = jnp.where(allowed, jnp.exp(scores - top), 0.0)
            total = lax.optimization_barrier(jnp.sum(weights, axis=1, keepdims=True))
            mixed = jnp.dot(weights.astype(jnp.bfloat16), value_head, preferred_element_type=jnp.float32)
            return mixed / total
        return lax.map(one_head, (query_block, key_heads, value_heads))
    outputs = lax.map(one_block, (query_blocks, block_starts))
    attended = outputs.transpose(0, 2, 1, 3).reshape(TOKENS, HEADS * HD).astype(jnp.bfloat16)
    group = HEADS * HD // N_HEAD
    summed = jnp.zeros((TOKENS, D), jnp.float32)
    for index in range(N_HEAD):
        partial_rows = jnp.dot(attended[:, index * group:(index + 1) * group], w_out[index * group:(index + 1) * group], preferred_element_type=jnp.float32).astype(jnp.bfloat16)
        partial_rows = lax.optimization_barrier(partial_rows)
        summed = summed + partial_rows.astype(jnp.float32)
    return summed.astype(jnp.bfloat16)
```

```python
import functools
import math

import jax
import jax.numpy as jnp
from jax import lax
from jax.experimental import pallas as pl
from jax.experimental.pallas import tpu as pltpu
from jax.sharding import PartitionSpec as P

HD = 128
BLOCKS = 8
RING = 4
MASKED = -1e30
FLOOR = -1e29
MESH = pl.DeviceIdType.MESH


def kernel(
    lengths_ref, q_ref, k_ref, v_ref, w_ref, out_ref,
    q_in, kv_in, q_two, keys_across, low, top, accum, scores, shares, mixed, gathered, weights, total,
    send_sem, q_sem, kv_sem, share_send, share_sem, mixed_send, mixed_sem,
    w_send, w_sem, across_send, across_sem, ring_send, ring_sem, relay_send, relay_sem, pair_send, pair_sem,
):
    rows = q_ref.shape[0]
    part = rows // 2
    heads = q_ref.shape[1] // HD
    width = heads * HD
    out_cols = out_ref.shape[1]
    ctx, head = lax.axis_index("ctx"), lax.axis_index("head")
    half, place = ctx // BLOCKS, lax.rem(ctx, BLOCKS)
    place_x, place_y = place // RING, lax.rem(place, RING)
    z, core = head // 2, lax.rem(head, 2)
    other = 1 - core
    first = half * BLOCKS
    sibling = (ctx, z * 2 + other)
    z_up, z_down, z_far = lax.rem(z + 1, RING), lax.rem(z + 3, RING), lax.rem(z + 2, RING)
    works = place_y < heads
    partner = ((RING - 1 - ctx // RING) * RING + place_y, head)

    barrier = pltpu.get_barrier_semaphore()
    for block in range(BLOCKS):
        for c in range(2):
            @pl.when((block != place) | (c != core))
            def _():
                pl.semaphore_signal(
                    barrier, inc=1, device_id=(first + block, z * 2 + c), device_id_type=MESH
                )
    for away in range(1, RING):
        for c in range(2):
            pl.semaphore_signal(
                barrier, inc=1, device_id=(ctx, lax.rem(z + away, RING) * 2 + c), device_id_type=MESH
            )
    pl.semaphore_signal(barrier, inc=1, device_id=partner, device_id_type=MESH)
    pl.semaphore_wait(barrier, 2 * BLOCKS - 1 + 2 * (RING - 1) + 1)

    def outgoing(away, c, n):
        local = lax.rem(place_y + away, RING)
        target = core * RING + local
        cols = pl.ds(pl.multiple_of(local * HD, HD), HD)
        span = pl.ds(c * part, part)
        source, dest, sem = (
            (k_ref, kv_in.at[place, 0, span], kv_sem.at[place]),
            (v_ref, kv_in.at[place, 1, span], kv_sem.at[place]),
            (q_ref, q_in.at[place], q_sem.at[place]),
        )[n]
        here = target == place

        def remote():
            return pltpu.make_async_remote_copy(
                src_ref=source.at[span, cols], dst_ref=dest, send_sem=send_sem.at[away, c, n], recv_sem=sem,
                device_id=(first + target, z * 2 + c), device_id_type=MESH,
            )

        def start():
            if away == 0:
                @pl.when((local < heads) & here & (core == c))
                def _():
                    pltpu.make_async_copy(source.at[span, cols], dest, sem).start()

                @pl.when((local < heads) & jnp.logical_not(here & (core == c)))
                def _():
                    remote().start()
            else:
                @pl.when(local < heads)
                def _():
                    remote().start()

        def finish():
            sent = local < heads
            if away == 0:
                sent &= jnp.logical_not(here & (core == c))

            @pl.when(sent)
            def _():
                remote().wait_send()

        return start, finish

    def weight_cols(target):
        return pl.ds(pl.multiple_of(target * out_cols, 128), out_cols)

    def weight_copy(away, c):
        target = lax.rem(z + away, RING) * 2 + c
        return pltpu.make_async_remote_copy(
            src_ref=w_ref.at[half, :, weight_cols(target)], dst_ref=weights.at[z, core, half],
            send_sem=w_send.at[away, c], recv_sem=w_sem.at[z, core],
            device_id=(ctx, target), device_id_type=MESH,
        )

    def weight_pair():
        return pltpu.make_async_remote_copy(
            src_ref=w_ref.at[:, :, weight_cols(z * 2 + other)], dst_ref=weights.at[z, core],
            send_sem=w_send.at[0, 0], recv_sem=w_sem.at[z, core],
            device_id=sibling, device_id_type=MESH,
        )

    def weight_across(away):
        piece = weights.at[lax.rem(z + away, RING), :, half]
        return pltpu.make_async_remote_copy(
            src_ref=piece, dst_ref=piece, send_sem=across_send.at[away], recv_sem=across_sem.at[away],
            device_id=partner, device_id_type=MESH,
        )

    def hand_across(away):
        source = lax.rem(z + away, RING)
        for c in range(2):
            piece = weights.at[source, c, half]
            pltpu.make_async_copy(piece, piece, w_sem.at[source, c]).wait()
        weight_across(away).start()

    def weights_here(away):
        source = lax.rem(z + away, RING)
        if away == 0:
            for c in range(2):
                piece = weights.at[source, c]
                pltpu.make_async_copy(piece, piece, w_sem.at[source, c]).wait()
        else:
            piece = weights.at[source, :, 1 - half]
            pltpu.make_async_copy(piece, piece, across_sem.at[away]).wait()

    sends = [[outgoing(away, c, n) for away in (1, 3, 2, 0) for c in range(2)] for n in range(3)]
    for group, away in zip(sends, (2, 1, 3)):
        for start, _ in group:
            start()
        for c in range(2):
            weight_copy(away, c).start()
    weight_pair().start()
    pltpu.make_async_copy(w_ref.at[:, :, weight_cols(head)], weights.at[z, core], w_sem.at[z, core]).start()

    scale = math.log2(math.e) / math.sqrt(HD)
    hh = heads * place_x + place_y

    def share(block):
        span = pl.ds(pl.multiple_of(core * part, 128), part)
        return pltpu.make_async_remote_copy(
            src_ref=kv_in.at[block, :, span], dst_ref=kv_in.at[block, :, span],
            send_sem=share_send.at[block], recv_sem=share_sem.at[block],
            device_id=sibling, device_id_type=MESH,
        )

    def shared(block):
        span = pl.ds(pl.multiple_of(other * part, 128), part)
        return pltpu.make_async_copy(
            kv_in.at[block, :, span], kv_in.at[block, :, span], share_sem.at[block]
        )

    def mixed_target(block):
        return gathered.at[
            z, pl.ds(pl.multiple_of(core * part, 128), part), pl.ds(pl.multiple_of(hh * HD, 128), HD)
        ]

    def mixed_copy(block):
        return pltpu.make_async_remote_copy(
            src_ref=mixed.at[block], dst_ref=mixed_target(block),
            send_sem=mixed_send.at[block], recv_sem=mixed_sem.at[hh],
            device_id=(first + block, head), device_id_type=MESH,
        )

    tile, group = part // 2, 16
    chunks = rows // HD

    def attend(pairs):
        tiles = [(pair, t) for pair in pairs for t in range(part // tile)]

        def score(n):
            (q_block, k_block, _), t = tiles[n]
            scores[n][...] = jnp.dot(
                q_two[q_block, pl.ds(t * tile, tile)], keys_across[k_block], preferred_element_type=jnp.float32
            )

        def soften(n):
            (q_block, k_block, diagonal), t = tiles[n]
            spans = [pl.ds(t * tile + g * group, group) for g in range(tile // group)]
            bounds = [low[q_block, span] - k_block * rows for span in spans]
            olds = [top[q_block, span] for span in spans]
            news = []
            for g, (bound, old) in enumerate(zip(bounds, olds)):
                parts = []
                for m in range(chunks):
                    lanes = lax.broadcasted_iota(jnp.int32, (group, HD), 1) + m * HD
                    allowed = lanes >= bound
                    if diagonal:
                        first_row = core * part + (t * tile + g * group)
                        allowed &= lanes <= lax.broadcasted_iota(jnp.int32, (group, HD), 0) + first_row
                    parts.append(jnp.where(allowed, scores[n][pl.ds(g * group, group), pl.ds(m * HD, HD)], MASKED))
                most = functools.reduce(jnp.maximum, parts)
                new = jnp.maximum(old, jnp.max(most, axis=1, keepdims=True))
                news.append(new)
                for m in range(chunks):
                    shares[n][pl.ds(g * group, group), pl.ds(m * HD, HD)] = jnp.exp2(parts[m] - new).astype(
                        jnp.bfloat16
                    )
            for span, new in zip(spans, news):
                top[q_block, span] = new
            return spans, olds, news

        def mix(n, state):
            (q_block, k_block, _), t = tiles[n]
            values = kv_in[k_block, 1]
            values = jnp.concatenate([values, jnp.ones_like(values)], axis=1)
            product = jnp.dot(shares[n][...], values, preferred_element_type=jnp.float32)
            factors = [jnp.exp2(old - new) for _, old, new in zip(*state)]
            sums = [
                accum[q_block, span] * jnp.concatenate([factor, factor], axis=1)
                for span, factor in zip(state[0], factors)
            ]
            for g, span in enumerate(state[0]):
                accum[q_block, span] = sums[g] + product[g * group : (g + 1) * group]

        score(0)
        for n in range(len(tiles)):
            if n + 1 < len(tiles):
                score(n + 1)
            mix(n, soften(n))

    @pl.when(works)
    def _():
        def blank(block, carry):
            positions = (
                lax.broadcasted_iota(jnp.int32, (part, HD), 0) + (half * BLOCKS + block) * rows + core * part
            )
            start = jnp.zeros((part, HD), jnp.int32)
            end = jnp.int32(0)
            for doc in range(lengths_ref.shape[0]):
                end = end + lengths_ref[doc]
                start = jnp.where(positions >= end, end, start)
            low[block] = start - half * BLOCKS * rows
            top[block] = jnp.full((part, HD), FLOOR, jnp.float32)
            accum[block] = jnp.zeros((part, 2 * HD), jnp.float32)
            return carry

        lax.fori_loop(0, BLOCKS, blank, 0)

        def block_at(step):
            dx = jnp.where((step == 3) | (step == 4) | (step == 5) | (step == 7), 1, 0)
            dy = jnp.where(
                (step == 1) | (step == 4), 1, jnp.where((step == 2) | (step == 5), 3, jnp.where(step >= 6, 2, 0))
            )
            return lax.rem(place_x + dx, 2) * RING + lax.rem(place_y + dy, RING)

        def receive(step):
            block = block_at(step)
            span = pl.ds(pl.multiple_of(core * part, 128), part)
            arrived = kv_in.at[block, :, span]
            pltpu.make_async_copy(arrived, arrived, kv_sem.at[block]).wait()
            share(block).start()

        ahead = BLOCKS - 2
        receive(0)

        def take(step, carry):
            for late, away in zip(range(BLOCKS - 3, BLOCKS), (1, 3, 2)):
                @pl.when(step == late)
                def _():
                    hand_across(away)

            @pl.when(step < ahead)
            def _():
                receive(step + 1)

            @pl.when(step > ahead)
            def _():
                receive(step)

            block = block_at(step)
            pltpu.make_async_copy(q_in.at[block], q_in.at[block], q_sem.at[block]).wait()
            scaled = q_in[block].astype(jnp.float32) * scale
            upper = scaled.astype(jnp.bfloat16)
            lower = (scaled - upper.astype(jnp.float32)).astype(jnp.bfloat16)
            q_two[block] = jnp.concatenate([upper, lower], axis=1)
            shared(block).wait()
            across = kv_in[block, 0].T
            keys_across[block] = jnp.concatenate([across, across], axis=0)

            def with_past(before):
                past = block_at(before)
                return jnp.maximum(block, past), jnp.minimum(block, past), False

            def two_at_once(count, inner):
                attend([with_past(2 * count), with_past(2 * count + 1)])
                return inner

            lax.fori_loop(0, step // 2, two_at_once, 0)

            @pl.when(lax.rem(step, 2) == 1)
            def _():
                attend([with_past(step - 1), (block, block, True)])

            @pl.when(lax.rem(step, 2) == 0)
            def _():
                attend([(block, block, True)])
            return carry

        lax.fori_loop(0, BLOCKS, take, 0)

        def finish(count, carry):
            block = block_at(BLOCKS - 1 - count)
            result = accum[block]
            mixed[block] = (result[:, :HD] / result[:, HD:]).astype(jnp.bfloat16)

            @pl.when(block == place)
            def _():
                pltpu.make_async_copy(mixed.at[block], mixed_target(block), mixed_sem.at[hh]).start()

            @pl.when(block != place)
            def _():
                mixed_copy(block).start()
            return carry

        lax.fori_loop(0, BLOCKS, finish, 0)

    @pl.when(jnp.logical_not(works))
    def _():
        for away in (1, 3, 2):
            hand_across(away)

    mine = pl.ds(pl.multiple_of(core * part, 128), part)
    theirs = pl.ds(pl.multiple_of(other * part, 128), part)
    halfway = part // 2
    lower_rows = pl.ds(pl.multiple_of(core * part, 128), halfway)
    upper_rows = pl.ds(pl.multiple_of(core * part + halfway, 128), halfway)

    order = [(dx, dy) for dy in (2, 1, 3, 0) for dx in (1, 0)]

    def each(action):
        for dx, dy in order:
            row, local = lax.rem(place_x + dx, 2), lax.rem(place_y + dy, RING)

            @pl.when(local < heads)
            def _():
                action(heads * row + local)

    def piece_of(source, span, piece):
        return gathered.at[source, span, pl.ds(pl.multiple_of(piece * HD, HD), HD)]

    def ring(source, span, piece, target, send, recv):
        return pltpu.make_async_remote_copy(
            src_ref=piece_of(source, span, piece), dst_ref=piece_of(source, span, piece),
            send_sem=send.at[piece], recv_sem=recv.at[piece],
            device_id=(ctx, target * 2 + core), device_id_type=MESH,
        )

    def to_pair(source, piece):
        return pltpu.make_async_remote_copy(
            src_ref=piece_of(source, mine, piece), dst_ref=piece_of(source, mine, piece),
            send_sem=pair_send.at[source, piece], recv_sem=pair_sem.at[source],
            device_id=sibling, device_id_type=MESH,
        )

    def piece_landed(source, span, piece, sem):
        here = piece_of(source, span, piece)
        pltpu.make_async_copy(here, here, sem.at[piece]).wait()

    def up(piece):
        return ring(z, mine, piece, z_up, ring_send.at[0], ring_sem.at[0])

    def down(piece):
        return ring(z, mine, piece, z_down, ring_send.at[1], ring_sem.at[1])

    def relay_up(piece):
        return ring(z_down, lower_rows, piece, z_up, relay_send.at[0], relay_sem.at[0])

    def relay_down(piece):
        return ring(z_up, upper_rows, piece, z_down, relay_send.at[1], relay_sem.at[1])

    def landed(source, span, sem):
        return pltpu.make_async_copy(gathered.at[source, span], gathered.at[source, span], sem)

    def project(away, start, last):
        source = lax.rem(z + away, RING)
        landed(source, theirs, pair_sem.at[source]).wait()
        weights_here(away)
        tile = rows // 4

        def some_rows(n, carry):
            span = pl.ds(pl.multiple_of(n * tile, 128), tile)
            product = jnp.dot(gathered[source, span], weights[source].reshape(2 * width, out_cols), preferred_element_type=jnp.float32)
            if not start:
                product = product + total[span]
            if last:
                out_ref[span] = product.astype(jnp.bfloat16)
            else:
                total[span] = product
            return carry

        lax.fori_loop(0, 4, some_rows, 0)

    def send_own(piece):
        piece_landed(z, mine, piece, mixed_sem)
        up(piece).start()
        down(piece).start()
        to_pair(z, piece).start()

    def pass_on(piece):
        piece_landed(z_down, mine, piece, ring_sem.at[0])
        relay_up(piece).start()
        to_pair(z_down, piece).start()
        piece_landed(z_up, mine, piece, ring_sem.at[1])
        relay_down(piece).start()
        to_pair(z_up, piece).start()

    def take_far(piece):
        piece_landed(z_far, lower_rows, piece, relay_sem.at[0])
        piece_landed(z_far, upper_rows, piece, relay_sem.at[1])
        to_pair(z_far, piece).start()

    each(send_own)
    project(0, True, False)
    each(pass_on)
    project(3, False, False)
    project(1, False, False)
    each(take_far)
    project(2, False, True)

    def all_left(piece):
        for copy in (up(piece), down(piece), relay_up(piece), relay_down(piece)):
            copy.wait_send()
        for source in range(RING):
            to_pair(source, piece).wait_send()

    each(all_left)
    for away in (2, 1, 3):
        for c in range(2):
            weight_copy(away, c).wait_send()
        weight_across(away).wait_send()
    weight_pair().wait_send()
    for group in sends:
        for _, finish in group:
            finish()

    @pl.when(works)
    def _():
        def left(block, carry):
            share(block).wait_send()

            @pl.when(block != place)
            def _():
                mixed_copy(block).wait_send()
            return carry

        lax.fori_loop(0, BLOCKS, left, 0)


def per_device(query, keys, values, doc_lengths, w_out):
    rows, width = query.shape
    heads = width // HD
    part = rows // 2
    out_cols = w_out.shape[1] // lax.axis_size("head")
    dma = pltpu.SemaphoreType.DMA
    pairs = BLOCKS * (BLOCKS + 1) // 2
    flops = pairs * part * rows * 4 * HD + 2 * rows * w_out.shape[1] * width
    return pl.pallas_call(
        kernel,
        out_shape=jax.ShapeDtypeStruct((rows, out_cols), jnp.bfloat16),
        in_specs=[pl.BlockSpec(memory_space=pltpu.SMEM)] + [pl.BlockSpec(memory_space=pl.ANY)] * 4,
        out_specs=pl.BlockSpec(memory_space=pltpu.VMEM),
        scratch_shapes=[
            pltpu.VMEM((BLOCKS, part, HD), jnp.bfloat16),
            pltpu.VMEM((BLOCKS, 2, rows, HD), jnp.bfloat16),
            pltpu.VMEM((BLOCKS, part, 2 * HD), jnp.bfloat16),
            pltpu.VMEM((BLOCKS, 2 * HD, rows), jnp.bfloat16),
            pltpu.VMEM((BLOCKS, part, HD), jnp.int32),
            pltpu.VMEM((BLOCKS, part, HD), jnp.float32),
            pltpu.VMEM((BLOCKS, part, 2 * HD), jnp.float32),
            [pltpu.VMEM((part // 2, rows), jnp.float32)] * 4,
            [pltpu.VMEM((part // 2, rows), jnp.bfloat16)] * 4,
            pltpu.VMEM((BLOCKS, part, HD), jnp.bfloat16),
            pltpu.VMEM((RING, rows, 2 * width), jnp.bfloat16),
            pltpu.VMEM((RING, 2, 2, width // 2, out_cols), jnp.bfloat16),
            pltpu.VMEM((rows, out_cols), jnp.float32),
            dma((RING, 2, 3)),
            dma((BLOCKS,)),
            dma((BLOCKS,)),
            dma((BLOCKS,)),
            dma((BLOCKS,)),
            dma((BLOCKS,)),
            dma((2 * heads,)),
            dma((RING, 2)),
            dma((RING, 2)),
            dma((RING,)),
            dma((RING,)),
            dma((2, 2 * heads)),
            dma((2, 2 * heads)),
            dma((2, 2 * heads)),
            dma((2, 2 * heads)),
            dma((RING, 2 * heads)),
            dma((RING,)),
        ],
        compiler_params=pltpu.CompilerParams(
            collective_id=0, has_side_effects=True, vmem_limit_bytes=56 * 1024 * 1024
        ),
        cost_estimate=pl.CostEstimate(
            flops=flops, bytes_accessed=16 * 1024 * 1024, transcendentals=pairs * part * rows
        ),
    )(doc_lengths, query, keys, values, w_out.reshape(2, width // 2, w_out.shape[1]))


def solution(mesh):
    return jax.shard_map(
        per_device,
        mesh=mesh,
        in_specs=(P("ctx", "head"), P("ctx", "head"), P("ctx", "head"), P(), P("head", None)),
        out_specs=P("ctx", "head"),
        check_vma=False,
    )
```

```python
import functools
import math

import jax
import jax.numpy as jnp
from jax import lax
from jax.experimental import pallas as pl
from jax.experimental.pallas import tpu as pltpu
from jax.sharding import PartitionSpec as P

HD = 128
BLOCKS = 8
RING = 4
OTHER_DOC = -(2.0**20)
FLOOR = -5e5
MESH = pl.DeviceIdType.MESH


def kernel(
    lengths_ref, q_ref, k_ref, v_ref, w_ref, out_ref,
    q_in, kv_in, q_two, keys_across, top, accum, scores, shares, mixed, gathered, weights, total,
    send_sem, q_sem, kv_sem, share_send, share_sem, mixed_send, mixed_sem,
    w_send, w_sem, across_send, across_sem, ring_send, ring_sem, relay_send, relay_sem, pair_send, pair_sem,
):
    rows = q_ref.shape[0]
    part = rows // 2
    heads = q_ref.shape[1] // HD
    width = heads * HD
    out_cols = out_ref.shape[1]
    ctx, head = lax.axis_index("ctx"), lax.axis_index("head")
    half, place = ctx // BLOCKS, lax.rem(ctx, BLOCKS)
    place_x, place_y = place // RING, lax.rem(place, RING)
    z, core = head // 2, lax.rem(head, 2)
    other = 1 - core
    first = half * BLOCKS
    sibling = (ctx, z * 2 + other)
    z_up, z_down, z_far = lax.rem(z + 1, RING), lax.rem(z + 3, RING), lax.rem(z + 2, RING)
    works = place_y < heads
    partner = ((RING - 1 - ctx // RING) * RING + place_y, head)

    barrier = pltpu.get_barrier_semaphore()
    for block in range(BLOCKS):
        for c in range(2):
            @pl.when((block != place) | (c != core))
            def _():
                pl.semaphore_signal(
                    barrier, inc=1, device_id=(first + block, z * 2 + c), device_id_type=MESH
                )
    for away in range(1, RING):
        for c in range(2):
            pl.semaphore_signal(
                barrier, inc=1, device_id=(ctx, lax.rem(z + away, RING) * 2 + c), device_id_type=MESH
            )
    pl.semaphore_signal(barrier, inc=1, device_id=partner, device_id_type=MESH)
    pl.semaphore_wait(barrier, 2 * BLOCKS - 1 + 2 * (RING - 1) + 1)

    def outgoing(away, c, n):
        local = lax.rem(place_y + away, RING)
        target = core * RING + local
        cols = pl.ds(pl.multiple_of(local * HD, HD), HD)
        span = pl.ds(c * part, part)
        source, dest, sem = (
            (k_ref, kv_in.at[place, 0, span], kv_sem.at[place]),
            (v_ref, kv_in.at[place, 1, span], kv_sem.at[place]),
            (q_ref, q_in.at[place], q_sem.at[place]),
        )[n]
        here = target == place

        def remote():
            return pltpu.make_async_remote_copy(
                src_ref=source.at[span, cols], dst_ref=dest, send_sem=send_sem.at[away, c, n], recv_sem=sem,
                device_id=(first + target, z * 2 + c), device_id_type=MESH,
            )

        def start():
            if away == 0:
                @pl.when((local < heads) & here & (core == c))
                def _():
                    pltpu.make_async_copy(source.at[span, cols], dest, sem).start()

                @pl.when((local < heads) & jnp.logical_not(here & (core == c)))
                def _():
                    remote().start()
            else:
                @pl.when(local < heads)
                def _():
                    remote().start()

        def finish():
            sent = local < heads
            if away == 0:
                sent &= jnp.logical_not(here & (core == c))

            @pl.when(sent)
            def _():
                remote().wait_send()

        return start, finish

    def weight_cols(target):
        return pl.ds(pl.multiple_of(target * out_cols, 128), out_cols)

    def weight_copy(away, c):
        target = lax.rem(z + away, RING) * 2 + c
        return pltpu.make_async_remote_copy(
            src_ref=w_ref.at[half, :, weight_cols(target)], dst_ref=weights.at[z, core, half],
            send_sem=w_send.at[away, c], recv_sem=w_sem.at[z, core],
            device_id=(ctx, target), device_id_type=MESH,
        )

    def weight_pair():
        return pltpu.make_async_remote_copy(
            src_ref=w_ref.at[:, :, weight_cols(z * 2 + other)], dst_ref=weights.at[z, core],
            send_sem=w_send.at[0, 0], recv_sem=w_sem.at[z, core],
            device_id=sibling, device_id_type=MESH,
        )

    def weight_across(away):
        piece = weights.at[lax.rem(z + away, RING), :, half]
        return pltpu.make_async_remote_copy(
            src_ref=piece, dst_ref=piece, send_sem=across_send.at[away], recv_sem=across_sem.at[away],
            device_id=partner, device_id_type=MESH,
        )

    def hand_across(away):
        source = lax.rem(z + away, RING)
        for c in range(2):
            piece = weights.at[source, c, half]
            pltpu.make_async_copy(piece, piece, w_sem.at[source, c]).wait()
        weight_across(away).start()

    def weights_here(away):
        source = lax.rem(z + away, RING)
        if away == 0:
            for c in range(2):
                piece = weights.at[source, c]
                pltpu.make_async_copy(piece, piece, w_sem.at[source, c]).wait()
        else:
            piece = weights.at[source, :, 1 - half]
            pltpu.make_async_copy(piece, piece, across_sem.at[away]).wait()

    sends = [[outgoing(away, c, n) for away in (1, 3, 2, 0) for c in range(2)] for n in range(3)]
    for group, away in zip(sends, (2, 1, 3)):
        for start, _ in group:
            start()
        for c in range(2):
            weight_copy(away, c).start()
    weight_pair().start()
    pltpu.make_async_copy(w_ref.at[:, :, weight_cols(head)], weights.at[z, core], w_sem.at[z, core]).start()

    scale = math.log2(math.e) / math.sqrt(HD)
    hh = heads * place_x + place_y

    def share(block):
        span = pl.ds(pl.multiple_of(core * part, 128), part)
        return pltpu.make_async_remote_copy(
            src_ref=kv_in.at[block, :, span], dst_ref=kv_in.at[block, :, span],
            send_sem=share_send.at[block], recv_sem=share_sem.at[block],
            device_id=sibling, device_id_type=MESH,
        )

    def shared(block):
        span = pl.ds(pl.multiple_of(other * part, 128), part)
        return pltpu.make_async_copy(
            kv_in.at[block, :, span], kv_in.at[block, :, span], share_sem.at[block]
        )

    def mixed_target(block):
        return gathered.at[
            z, pl.ds(pl.multiple_of(core * part, 128), part), pl.ds(pl.multiple_of(hh * HD, 128), HD)
        ]

    def mixed_copy(block):
        return pltpu.make_async_remote_copy(
            src_ref=mixed.at[block], dst_ref=mixed_target(block),
            send_sem=mixed_send.at[block], recv_sem=mixed_sem.at[hh],
            device_id=(first + block, head), device_id_type=MESH,
        )

    tile, group = part, 16
    chunks = rows // HD

    def attend(pairs):
        tiles = [(pair, t) for pair in pairs for t in range(part // tile)]

        def score(n):
            (q_block, k_block, _), t = tiles[n]
            scores[n][...] = jnp.dot(
                q_two[q_block, pl.ds(t * tile, tile)], keys_across[k_block], preferred_element_type=jnp.float32
            )

        def soften(n):
            (q_block, k_block, diagonal), t = tiles[n]
            spans = [pl.ds(t * tile + g * group, group) for g in range(tile // group)]
            olds = [top[q_block, span] for span in spans]
            news = []
            for g, old in enumerate(olds):
                parts = []
                for m in range(chunks):
                    piece = scores[n][pl.ds(g * group, group), pl.ds(m * HD, HD)]
                    if diagonal:
                        lanes = lax.broadcasted_iota(jnp.int32, (group, HD), 1) + m * HD
                        first_row = core * part + (t * tile + g * group)
                        allowed = lanes <= lax.broadcasted_iota(jnp.int32, (group, HD), 0) + first_row
                        piece = jnp.where(allowed, piece, OTHER_DOC)
                    parts.append(piece)
                most = functools.reduce(jnp.maximum, parts)
                new = jnp.maximum(old, jnp.max(most, axis=1, keepdims=True))
                news.append(new)
                for m in range(chunks):
                    shares[n][pl.ds(g * group, group), pl.ds(m * HD, HD)] = jnp.exp2((parts[m] - new) * scale).astype(
                        jnp.bfloat16
                    )
            for span, new in zip(spans, news):
                top[q_block, span] = new
            return spans, olds, news

        def mix(n, state):
            (q_block, k_block, _), t = tiles[n]
            values = kv_in[k_block, 1]
            values = jnp.concatenate([values, jnp.ones_like(values)], axis=1)
            product = jnp.dot(shares[n][...], values, preferred_element_type=jnp.float32)
            factors = [jnp.exp2((old - new) * scale) for _, old, new in zip(*state)]
            sums = [
                accum[q_block, span] * jnp.concatenate([factor, factor], axis=1)
                for span, factor in zip(state[0], factors)
            ]
            for g, span in enumerate(state[0]):
                accum[q_block, span] = sums[g] + product[g * group : (g + 1) * group]

        score(0)
        for n in range(len(tiles)):
            if n + 1 < len(tiles):
                score(n + 1)
            mix(n, soften(n))

    @pl.when(works)
    def _():
        def doc_at(positions):
            doc, end = jnp.zeros_like(positions), jnp.int32(0)
            for n in range(lengths_ref.shape[0]):
                end = end + lengths_ref[n]
                doc = jnp.where(positions >= end, n + 1, doc)
            return doc

        def blank(block, carry):
            start = (half * BLOCKS + block) * rows
            q_doc = doc_at(lax.broadcasted_iota(jnp.int32, (part, HD), 0) + (start + core * part))
            same = lax.broadcasted_iota(jnp.int32, (part, HD), 1) == q_doc
            q_two[block, :, pl.ds(HD, HD)] = jnp.where(same, 0.0, OTHER_DOC).astype(jnp.bfloat16)
            k_doc = doc_at(lax.broadcasted_iota(jnp.int32, (HD, rows), 1) + start)
            same = lax.broadcasted_iota(jnp.int32, (HD, rows), 0) == k_doc
            keys_across[block, pl.ds(HD, HD)] = jnp.where(same, 1.0, 0.0).astype(jnp.bfloat16)
            top[block] = jnp.full((part, HD), FLOOR, jnp.float32)
            accum[block] = jnp.zeros((part, 2 * HD), jnp.float32)
            return carry

        lax.fori_loop(0, BLOCKS, blank, 0)

        def block_at(step):
            dx = jnp.where((step == 3) | (step == 4) | (step == 5) | (step == 7), 1, 0)
            dy = jnp.where(
                (step == 1) | (step == 4), 1, jnp.where((step == 2) | (step == 5), 3, jnp.where(step >= 6, 2, 0))
            )
            return lax.rem(place_x + dx, 2) * RING + lax.rem(place_y + dy, RING)

        def receive(step):
            block = block_at(step)
            span = pl.ds(pl.multiple_of(core * part, 128), part)
            arrived = kv_in.at[block, :, span]
            pltpu.make_async_copy(arrived, arrived, kv_sem.at[block]).wait()
            share(block).start()

        ahead = BLOCKS - 2
        receive(0)

        def take(step, carry):
            for late, away in zip(range(BLOCKS - 3, BLOCKS), (1, 3, 2)):
                @pl.when(step == late)
                def _():
                    hand_across(away)

            @pl.when(step < ahead)
            def _():
                receive(step + 1)

            @pl.when(step > ahead)
            def _():
                receive(step)

            block = block_at(step)
            pltpu.make_async_copy(q_in.at[block], q_in.at[block], q_sem.at[block]).wait()
            q_two[block, :, pl.ds(0, HD)] = q_in[block]
            shared(block).wait()
            keys_across[block, pl.ds(0, HD)] = kv_in[block, 0].T

            def with_past(before):
                past = block_at(before)
                return jnp.maximum(block, past), jnp.minimum(block, past), False

            def two_at_once(count, inner):
                attend([with_past(2 * count), with_past(2 * count + 1)])
                return inner

            lax.fori_loop(0, step // 2, two_at_once, 0)

            @pl.when(lax.rem(step, 2) == 1)
            def _():
                attend([with_past(step - 1), (block, block, True)])

            @pl.when(lax.rem(step, 2) == 0)
            def _():
                attend([(block, block, True)])
            return carry

        lax.fori_loop(0, BLOCKS, take, 0)

        def finish(count, carry):
            block = block_at(BLOCKS - 1 - count)
            result = accum[block]
            mixed[block] = (result[:, :HD] / result[:, HD:]).astype(jnp.bfloat16)

            @pl.when(block == place)
            def _():
                pltpu.make_async_copy(mixed.at[block], mixed_target(block), mixed_sem.at[hh]).start()

            @pl.when(block != place)
            def _():
                mixed_copy(block).start()
            return carry

        lax.fori_loop(0, BLOCKS, finish, 0)

    @pl.when(jnp.logical_not(works))
    def _():
        for away in (1, 3, 2):
            hand_across(away)

    mine = pl.ds(pl.multiple_of(core * part, 128), part)
    theirs = pl.ds(pl.multiple_of(other * part, 128), part)
    halfway = part // 2
    lower_rows = pl.ds(pl.multiple_of(core * part, 128), halfway)
    upper_rows = pl.ds(pl.multiple_of(core * part + halfway, 128), halfway)

    order = [(dx, dy) for dy in (2, 1, 3, 0) for dx in (1, 0)]

    def each(action):
        for dx, dy in order:
            row, local = lax.rem(place_x + dx, 2), lax.rem(place_y + dy, RING)

            @pl.when(local < heads)
            def _():
                action(heads * row + local)

    def piece_of(source, span, piece):
        return gathered.at[source, span, pl.ds(pl.multiple_of(piece * HD, HD), HD)]

    def ring(source, span, piece, target, send, recv):
        return pltpu.make_async_remote_copy(
            src_ref=piece_of(source, span, piece), dst_ref=piece_of(source, span, piece),
            send_sem=send.at[piece], recv_sem=recv.at[piece],
            device_id=(ctx, target * 2 + core), device_id_type=MESH,
        )

    def to_pair(source, piece):
        return pltpu.make_async_remote_copy(
            src_ref=piece_of(source, mine, piece), dst_ref=piece_of(source, mine, piece),
            send_sem=pair_send.at[source, piece], recv_sem=pair_sem.at[source],
            device_id=sibling, device_id_type=MESH,
        )

    def piece_landed(source, span, piece, sem):
        here = piece_of(source, span, piece)
        pltpu.make_async_copy(here, here, sem.at[piece]).wait()

    def up(piece):
        return ring(z, mine, piece, z_up, ring_send.at[0], ring_sem.at[0])

    def down(piece):
        return ring(z, mine, piece, z_down, ring_send.at[1], ring_sem.at[1])

    def relay_up(piece):
        return ring(z_down, lower_rows, piece, z_up, relay_send.at[0], relay_sem.at[0])

    def relay_down(piece):
        return ring(z_up, upper_rows, piece, z_down, relay_send.at[1], relay_sem.at[1])

    def landed(source, span, sem):
        return pltpu.make_async_copy(gathered.at[source, span], gathered.at[source, span], sem)

    def project(away, start, last):
        source = lax.rem(z + away, RING)
        landed(source, theirs, pair_sem.at[source]).wait()
        weights_here(away)
        tile = rows // 4

        def some_rows(n, carry):
            span = pl.ds(pl.multiple_of(n * tile, 128), tile)
            product = jnp.dot(gathered[source, span], weights[source].reshape(2 * width, out_cols), preferred_element_type=jnp.float32)
            if not start:
                product = product + total[span]
            if last:
                out_ref[span] = product.astype(jnp.bfloat16)
            else:
                total[span] = product
            return carry

        lax.fori_loop(0, 4, some_rows, 0)

    def send_own(piece):
        piece_landed(z, mine, piece, mixed_sem)
        up(piece).start()
        down(piece).start()
        to_pair(z, piece).start()

    def pass_on(piece):
        piece_landed(z_down, mine, piece, ring_sem.at[0])
        relay_up(piece).start()
        to_pair(z_down, piece).start()
        piece_landed(z_up, mine, piece, ring_sem.at[1])
        relay_down(piece).start()
        to_pair(z_up, piece).start()

    def take_far(piece):
        piece_landed(z_far, lower_rows, piece, relay_sem.at[0])
        piece_landed(z_far, upper_rows, piece, relay_sem.at[1])
        to_pair(z_far, piece).start()

    each(send_own)
    project(0, True, False)
    each(pass_on)
    project(3, False, False)
    project(1, False, False)
    each(take_far)
    project(2, False, True)

    def all_left(piece):
        for copy in (up(piece), down(piece), relay_up(piece), relay_down(piece)):
            copy.wait_send()
        for source in range(RING):
            to_pair(source, piece).wait_send()

    each(all_left)
    for away in (2, 1, 3):
        for c in range(2):
            weight_copy(away, c).wait_send()
        weight_across(away).wait_send()
    weight_pair().wait_send()
    for group in sends:
        for _, finish in group:
            finish()

    @pl.when(works)
    def _():
        def left(block, carry):
            share(block).wait_send()

            @pl.when(block != place)
            def _():
                mixed_copy(block).wait_send()
            return carry

        lax.fori_loop(0, BLOCKS, left, 0)


def per_device(query, keys, values, doc_lengths, w_out):
    rows, width = query.shape
    heads = width // HD
    part = rows // 2
    out_cols = w_out.shape[1] // lax.axis_size("head")
    dma = pltpu.SemaphoreType.DMA
    pairs = BLOCKS * (BLOCKS + 1) // 2
    flops = pairs * part * rows * 4 * HD + 2 * rows * w_out.shape[1] * width
    return pl.pallas_call(
        kernel,
        out_shape=jax.ShapeDtypeStruct((rows, out_cols), jnp.bfloat16),
        in_specs=[pl.BlockSpec(memory_space=pltpu.SMEM)] + [pl.BlockSpec(memory_space=pl.ANY)] * 4,
        out_specs=pl.BlockSpec(memory_space=pltpu.VMEM),
        scratch_shapes=[
            pltpu.VMEM((BLOCKS, part, HD), jnp.bfloat16),
            pltpu.VMEM((BLOCKS, 2, rows, HD), jnp.bfloat16),
            pltpu.VMEM((BLOCKS, part, 2 * HD), jnp.bfloat16),
            pltpu.VMEM((BLOCKS, 2 * HD, rows), jnp.bfloat16),
            pltpu.VMEM((BLOCKS, part, HD), jnp.float32),
            pltpu.VMEM((BLOCKS, part, 2 * HD), jnp.float32),
            [pltpu.VMEM((part, rows), jnp.float32)] * 2,
            [pltpu.VMEM((part, rows), jnp.bfloat16)] * 2,
            pltpu.VMEM((BLOCKS, part, HD), jnp.bfloat16),
            pltpu.VMEM((RING, rows, 2 * width), jnp.bfloat16),
            pltpu.VMEM((RING, 2, 2, width // 2, out_cols), jnp.bfloat16),
            pltpu.VMEM((rows, out_cols), jnp.float32),
            dma((RING, 2, 3)),
            dma((BLOCKS,)),
            dma((BLOCKS,)),
            dma((BLOCKS,)),
            dma((BLOCKS,)),
            dma((BLOCKS,)),
            dma((2 * heads,)),
            dma((RING, 2)),
            dma((RING, 2)),
            dma((RING,)),
            dma((RING,)),
            dma((2, 2 * heads)),
            dma((2, 2 * heads)),
            dma((2, 2 * heads)),
            dma((2, 2 * heads)),
            dma((RING, 2 * heads)),
            dma((RING,)),
        ],
        compiler_params=pltpu.CompilerParams(
            collective_id=0, has_side_effects=True, vmem_limit_bytes=56 * 1024 * 1024
        ),
        cost_estimate=pl.CostEstimate(
            flops=flops, bytes_accessed=16 * 1024 * 1024, transcendentals=pairs * part * rows
        ),
    )(doc_lengths, query, keys, values, w_out.reshape(2, width // 2, w_out.shape[1]))


def solution(mesh):
    return jax.shard_map(
        per_device,
        mesh=mesh,
        in_specs=(P("ctx", "head"), P("ctx", "head"), P("ctx", "head"), P(), P("head", None)),
        out_specs=P("ctx", "head"),
        check_vma=False,
    )
```

```python
import functools
import math

import jax
import jax.numpy as jnp
from jax import lax
from jax.experimental import pallas as pl
from jax.experimental.pallas import tpu as pltpu
from jax.sharding import PartitionSpec as P

HD = 128
BLOCKS = 8
RING = 4
OTHER_DOC = -(2.0**20)
FLOOR = -5e5
MESH = pl.DeviceIdType.MESH


def kernel(
    lengths_ref, q_ref, k_ref, v_ref, w_ref, out_ref,
    q_in, kv_in, q_two, keys_across, top, accum, scores, shares, mixed, gathered, weights, total,
    send_sem, q_sem, kv_sem, share_send, share_sem, mixed_send, mixed_sem,
    w_send, w_sem, across_send, across_sem, ring_send, ring_sem, relay_send, relay_sem, pair_send, pair_sem,
):
    rows = q_ref.shape[0]
    part = rows // 2
    heads = q_ref.shape[1] // HD
    width = heads * HD
    out_cols = out_ref.shape[1]
    ctx, head = lax.axis_index("ctx"), lax.axis_index("head")
    half, place = ctx // BLOCKS, lax.rem(ctx, BLOCKS)
    place_x, place_y = place // RING, lax.rem(place, RING)
    z, core = head // 2, lax.rem(head, 2)
    other = 1 - core
    first = half * BLOCKS
    sibling = (ctx, z * 2 + other)
    z_up, z_down, z_far = lax.rem(z + 1, RING), lax.rem(z + 3, RING), lax.rem(z + 2, RING)
    works = place_y < heads
    partner = ((RING - 1 - ctx // RING) * RING + place_y, head)

    barrier = pltpu.get_barrier_semaphore()
    for block in range(BLOCKS):
        for c in range(2):
            @pl.when((block != place) | (c != core))
            def _():
                pl.semaphore_signal(
                    barrier, inc=1, device_id=(first + block, z * 2 + c), device_id_type=MESH
                )
    for away in range(1, RING):
        for c in range(2):
            pl.semaphore_signal(
                barrier, inc=1, device_id=(ctx, lax.rem(z + away, RING) * 2 + c), device_id_type=MESH
            )
    pl.semaphore_signal(barrier, inc=1, device_id=partner, device_id_type=MESH)
    pl.semaphore_wait(barrier, 2 * BLOCKS - 1 + 2 * (RING - 1) + 1)

    def outgoing(away, c, n):
        local = lax.rem(place_y + away, RING)
        target = core * RING + local
        cols = pl.ds(pl.multiple_of(local * HD, HD), HD)
        span = pl.ds(c * part, part)
        source, dest, sem = (
            (k_ref, kv_in.at[place, 0, span], kv_sem.at[place]),
            (v_ref, kv_in.at[place, 1, span], kv_sem.at[place]),
            (q_ref, q_in.at[place], q_sem.at[place]),
        )[n]
        here = target == place

        def remote():
            return pltpu.make_async_remote_copy(
                src_ref=source.at[span, cols], dst_ref=dest, send_sem=send_sem.at[away, c, n], recv_sem=sem,
                device_id=(first + target, z * 2 + c), device_id_type=MESH,
            )

        def start():
            if away == 0:
                @pl.when((local < heads) & here & (core == c))
                def _():
                    pltpu.make_async_copy(source.at[span, cols], dest, sem).start()

                @pl.when((local < heads) & jnp.logical_not(here & (core == c)))
                def _():
                    remote().start()
            else:
                @pl.when(local < heads)
                def _():
                    remote().start()

        def finish():
            sent = local < heads
            if away == 0:
                sent &= jnp.logical_not(here & (core == c))

            @pl.when(sent)
            def _():
                remote().wait_send()

        return start, finish

    def weight_cols(target):
        return pl.ds(pl.multiple_of(target * out_cols, 128), out_cols)

    def weight_copy(away, c):
        target = lax.rem(z + away, RING) * 2 + c
        return pltpu.make_async_remote_copy(
            src_ref=w_ref.at[half, :, weight_cols(target)], dst_ref=weights.at[z, core, half],
            send_sem=w_send.at[away, c], recv_sem=w_sem.at[z, core],
            device_id=(ctx, target), device_id_type=MESH,
        )

    def weight_pair():
        return pltpu.make_async_remote_copy(
            src_ref=w_ref.at[:, :, weight_cols(z * 2 + other)], dst_ref=weights.at[z, core],
            send_sem=w_send.at[0, 0], recv_sem=w_sem.at[z, core],
            device_id=sibling, device_id_type=MESH,
        )

    def weight_across(away):
        piece = weights.at[lax.rem(z + away, RING), :, half]
        return pltpu.make_async_remote_copy(
            src_ref=piece, dst_ref=piece, send_sem=across_send.at[away], recv_sem=across_sem.at[away],
            device_id=partner, device_id_type=MESH,
        )

    def hand_across(away):
        source = lax.rem(z + away, RING)
        for c in range(2):
            piece = weights.at[source, c, half]
            pltpu.make_async_copy(piece, piece, w_sem.at[source, c]).wait()
        weight_across(away).start()

    def weights_here(away):
        source = lax.rem(z + away, RING)
        if away == 0:
            for c in range(2):
                piece = weights.at[source, c]
                pltpu.make_async_copy(piece, piece, w_sem.at[source, c]).wait()
        else:
            piece = weights.at[source, :, 1 - half]
            pltpu.make_async_copy(piece, piece, across_sem.at[away]).wait()

    sends = [[outgoing(away, c, n) for away in (1, 3, 2, 0) for c in range(2)] for n in range(3)]
    for group, away in zip(sends, (2, 1, 3)):
        for start, _ in group:
            start()
        for c in range(2):
            weight_copy(away, c).start()
    weight_pair().start()
    pltpu.make_async_copy(w_ref.at[:, :, weight_cols(head)], weights.at[z, core], w_sem.at[z, core]).start()

    scale = math.log2(math.e) / math.sqrt(HD)
    hh = heads * place_x + place_y

    def share(block):
        span = pl.ds(pl.multiple_of(core * part, 128), part)
        return pltpu.make_async_remote_copy(
            src_ref=kv_in.at[block, :, span], dst_ref=kv_in.at[block, :, span],
            send_sem=share_send.at[block], recv_sem=share_sem.at[block],
            device_id=sibling, device_id_type=MESH,
        )

    def shared(block):
        span = pl.ds(pl.multiple_of(other * part, 128), part)
        return pltpu.make_async_copy(
            kv_in.at[block, :, span], kv_in.at[block, :, span], share_sem.at[block]
        )

    tile, group = part // 2, 16
    chunks = rows // HD

    def half_rows(c, t):
        return pl.ds(pl.multiple_of(c * part + t * tile, 128), tile)

    def mixed_target(t):
        return gathered.at[z, half_rows(core, t), pl.ds(pl.multiple_of(hh * HD, HD), HD)]

    def mixed_source(block, t):
        return mixed.at[block, pl.ds(pl.multiple_of(t * tile, 128), tile)]

    def mixed_copy(block, t):
        return pltpu.make_async_remote_copy(
            src_ref=mixed_source(block, t), dst_ref=mixed_target(t),
            send_sem=mixed_send.at[t, block], recv_sem=mixed_sem.at[t, hh],
            device_id=(first + block, head), device_id_type=MESH,
        )

    def finish(block, t):
        result = accum[block, pl.ds(pl.multiple_of(t * tile, 128), tile)]
        mixed[block, pl.ds(pl.multiple_of(t * tile, 128), tile)] = (
            result[:, :HD] / result[:, HD:]
        ).astype(jnp.bfloat16)

        @pl.when(block == place)
        def _():
            pltpu.make_async_copy(mixed_source(block, t), mixed_target(t), mixed_sem.at[t, hh]).start()

        @pl.when(block != place)
        def _():
            mixed_copy(block, t).start()

    def attend(tiles, t):
        first_row = pl.multiple_of(t * tile, 128)

        def score(n):
            q_block, k_block, _ = tiles[n]
            scores[n][...] = jnp.dot(
                q_two[q_block, pl.ds(first_row, tile)], keys_across[k_block], preferred_element_type=jnp.float32
            )

        def soften(n):
            q_block, k_block, diagonal = tiles[n]
            spans = [pl.ds(pl.multiple_of(first_row + g * group, group), group) for g in range(tile // group)]
            olds = [top[q_block, span] for span in spans]
            news = []
            for g, old in enumerate(olds):
                parts = []
                for m in range(chunks):
                    piece = scores[n][pl.ds(g * group, group), pl.ds(m * HD, HD)]
                    if diagonal:
                        lanes = lax.broadcasted_iota(jnp.int32, (group, HD), 1) + m * HD
                        row = core * part + first_row + g * group
                        allowed = lanes <= lax.broadcasted_iota(jnp.int32, (group, HD), 0) + row
                        piece = jnp.where(allowed, piece, OTHER_DOC)
                    parts.append(piece)
                most = functools.reduce(jnp.maximum, parts)
                new = jnp.maximum(old, jnp.max(most, axis=1, keepdims=True))
                news.append(new)
                for m in range(chunks):
                    shares[n][pl.ds(g * group, group), pl.ds(m * HD, HD)] = jnp.exp2((parts[m] - new) * scale).astype(
                        jnp.bfloat16
                    )
            for span, new in zip(spans, news):
                top[q_block, span] = new
            return spans, olds, news

        def mix(n, state):
            q_block, k_block, _ = tiles[n]
            values = kv_in[k_block, 1]
            values = jnp.concatenate([values, jnp.ones_like(values)], axis=1)
            product = jnp.dot(shares[n][...], values, preferred_element_type=jnp.float32)
            factors = [jnp.exp2((old - new) * scale) for _, old, new in zip(*state)]
            sums = [
                accum[q_block, span] * jnp.concatenate([factor, factor], axis=1)
                for span, factor in zip(state[0], factors)
            ]
            for g, span in enumerate(state[0]):
                accum[q_block, span] = sums[g] + product[g * group : (g + 1) * group]

        score(0)
        for n in range(len(tiles)):
            if n + 1 < len(tiles):
                score(n + 1)
            mix(n, soften(n))

    order = [(dx, dy) for dy in (2, 1, 3, 0) for dx in (1, 0)]

    def each(action, t):
        for dx, dy in order:
            row, local = lax.rem(place_x + dx, 2), lax.rem(place_y + dy, RING)

            @pl.when(local < heads)
            def _():
                action(heads * row + local, t)

    mine = [half_rows(core, t) for t in range(2)]
    theirs = [half_rows(other, t) for t in range(2)]
    far_rows = [
        [pl.ds(pl.multiple_of(core * part + t * tile + n * (tile // 2), 128), tile // 2) for n in range(2)]
        for t in range(2)
    ]

    def piece_of(source, span, piece):
        return gathered.at[source, span, pl.ds(pl.multiple_of(piece * HD, HD), HD)]

    def ring(source, span, piece, target, send, recv):
        return pltpu.make_async_remote_copy(
            src_ref=piece_of(source, span, piece), dst_ref=piece_of(source, span, piece),
            send_sem=send.at[piece], recv_sem=recv.at[piece],
            device_id=(ctx, target * 2 + core), device_id_type=MESH,
        )

    def to_pair(source, piece, t):
        return pltpu.make_async_remote_copy(
            src_ref=piece_of(source, mine[t], piece), dst_ref=piece_of(source, mine[t], piece),
            send_sem=pair_send.at[t, source, piece], recv_sem=pair_sem.at[t, source],
            device_id=sibling, device_id_type=MESH,
        )

    def piece_landed(source, span, piece, sem):
        here = piece_of(source, span, piece)
        pltpu.make_async_copy(here, here, sem.at[piece]).wait()

    def up(piece, t):
        return ring(z, mine[t], piece, z_up, ring_send.at[t, 0], ring_sem.at[t, 0])

    def down(piece, t):
        return ring(z, mine[t], piece, z_down, ring_send.at[t, 1], ring_sem.at[t, 1])

    def relay_up(piece, t):
        return ring(z_down, far_rows[t][0], piece, z_up, relay_send.at[t, 0], relay_sem.at[t, 0])

    def relay_down(piece, t):
        return ring(z_up, far_rows[t][1], piece, z_down, relay_send.at[t, 1], relay_sem.at[t, 1])

    def send_own(piece, t):
        piece_landed(z, mine[t], piece, mixed_sem.at[t])
        up(piece, t).start()
        down(piece, t).start()
        to_pair(z, piece, t).start()

    def pass_on(piece, t):
        piece_landed(z_down, mine[t], piece, ring_sem.at[t, 0])
        relay_up(piece, t).start()
        to_pair(z_down, piece, t).start()
        piece_landed(z_up, mine[t], piece, ring_sem.at[t, 1])
        relay_down(piece, t).start()
        to_pair(z_up, piece, t).start()

    def take_far(piece, t):
        piece_landed(z_far, far_rows[t][0], piece, relay_sem.at[t, 0])
        piece_landed(z_far, far_rows[t][1], piece, relay_sem.at[t, 1])
        to_pair(z_far, piece, t).start()

    @pl.when(works)
    def _():
        def doc_at(positions):
            doc, end = jnp.zeros_like(positions), jnp.int32(0)
            for n in range(lengths_ref.shape[0]):
                end = end + lengths_ref[n]
                doc = jnp.where(positions >= end, n + 1, doc)
            return doc

        def blank(block, carry):
            start = (half * BLOCKS + block) * rows
            q_doc = doc_at(lax.broadcasted_iota(jnp.int32, (part, HD), 0) + (start + core * part))
            same = lax.broadcasted_iota(jnp.int32, (part, HD), 1) == q_doc
            q_two[block, :, pl.ds(HD, HD)] = jnp.where(same, 0.0, OTHER_DOC).astype(jnp.bfloat16)
            k_doc = doc_at(lax.broadcasted_iota(jnp.int32, (HD, rows), 1) + start)
            same = lax.broadcasted_iota(jnp.int32, (HD, rows), 0) == k_doc
            keys_across[block, pl.ds(HD, HD)] = jnp.where(same, 1.0, 0.0).astype(jnp.bfloat16)
            top[block] = jnp.full((part, HD), FLOOR, jnp.float32)
            accum[block] = jnp.zeros((part, 2 * HD), jnp.float32)
            return carry

        lax.fori_loop(0, BLOCKS, blank, 0)

        def block_at(step):
            dx = jnp.where((step == 3) | (step == 4) | (step == 5) | (step == 7), 1, 0)
            dy = jnp.where(
                (step == 1) | (step == 4), 1, jnp.where((step == 2) | (step == 5), 3, jnp.where(step >= 6, 2, 0))
            )
            return lax.rem(place_x + dx, 2) * RING + lax.rem(place_y + dy, RING)

        def receive(step):
            block = block_at(step)
            span = pl.ds(pl.multiple_of(core * part, 128), part)
            arrived = kv_in.at[block, :, span]
            pltpu.make_async_copy(arrived, arrived, kv_sem.at[block]).wait()
            share(block).start()

        ahead = BLOCKS - 2
        receive(0)

        def take(turn, carry):
            t, step = turn // BLOCKS, lax.rem(turn, BLOCKS)
            for late, away in zip(range(BLOCKS - 3, BLOCKS), (1, 3, 2)):
                @pl.when(turn == late)
                def _():
                    hand_across(away)

            @pl.when(turn < ahead)
            def _():
                receive(turn + 1)

            @pl.when((turn > ahead) & (turn < BLOCKS))
            def _():
                receive(turn)

            block = jnp.where(t == 0, block_at(step), step)

            @pl.when(t == 0)
            def _():
                pltpu.make_async_copy(q_in.at[block], q_in.at[block], q_sem.at[block]).wait()
                q_two[block, :, pl.ds(0, HD)] = q_in[block]
                shared(block).wait()
                keys_across[block, pl.ds(0, HD)] = kv_in[block, 0].T

            def with_past(before):
                past = jnp.where(t == 0, block_at(before), before)
                return jnp.maximum(block, past), jnp.minimum(block, past), False

            def four_at_once(count, inner):
                attend([with_past(4 * count + n) for n in range(4)], t)
                return inner

            lax.fori_loop(0, step // 4, four_at_once, 0)
            for rest in range(4):
                @pl.when(lax.rem(step, 4) == rest)
                def _():
                    attend([with_past(step - 1 - n) for n in range(rest)] + [(block, block, True)], t)

            @pl.when(t == 1)
            def _():
                finish(block, 1)

            @pl.when(turn == BLOCKS - 1)
            def _():
                def finish_all(count, inner):
                    finish(block_at(BLOCKS - 1 - count), 0)
                    return inner

                lax.fori_loop(0, BLOCKS, finish_all, 0)

            for when, action in ((BLOCKS + 3, send_own), (BLOCKS + 5, pass_on), (BLOCKS + 6, take_far)):
                @pl.when(turn == when)
                def _():
                    each(action, 0)

            return carry

        lax.fori_loop(0, 2 * BLOCKS, take, 0)

    @pl.when(jnp.logical_not(works))
    def _():
        for away in (1, 3, 2):
            hand_across(away)
        for action in (send_own, pass_on, take_far):
            each(action, 0)

    def half_landed(away, t):
        source = lax.rem(z + away, RING)
        here = gathered.at[source, theirs[t]]
        pltpu.make_async_copy(here, here, pair_sem.at[t, source]).wait()

    def project(aways, t, start, last):
        def some_rows(c, carry):
            span = half_rows(c, t)
            product = None if start else total[pl.ds(pl.multiple_of(c * tile, 128), tile)]
            for away in aways:
                source = lax.rem(z + away, RING)
                term = jnp.dot(
                    gathered[source, span], weights[source].reshape(2 * width, out_cols),
                    preferred_element_type=jnp.float32,
                )
                product = term if product is None else product + term
            if last:
                out_ref[span] = product.astype(jnp.bfloat16)
            else:
                total[pl.ds(pl.multiple_of(c * tile, 128), tile)] = product
            return carry

        lax.fori_loop(0, 2, some_rows, 0)

    each(send_own, 1)
    for away in range(RING):
        half_landed(away, 0)
        weights_here(away)
    project((0, 1, 2, 3), 0, True, True)
    each(pass_on, 1)
    for away in (0, 1, 3):
        half_landed(away, 1)
    project((0, 1, 3), 1, True, False)
    each(take_far, 1)
    half_landed(2, 1)
    project((2,), 1, False, True)

    def all_left(piece, t):
        for copy in (up, down, relay_up, relay_down):
            copy(piece, t).wait_send()
        for source in range(RING):
            to_pair(source, piece, t).wait_send()

    for t in range(2):
        each(all_left, t)
    for away in (2, 1, 3):
        for c in range(2):
            weight_copy(away, c).wait_send()
        weight_across(away).wait_send()
    weight_pair().wait_send()
    for group in sends:
        for _, finish in group:
            finish()

    @pl.when(works)
    def _():
        def left(block, carry):
            share(block).wait_send()

            @pl.when(block != place)
            def _():
                for t in range(2):
                    mixed_copy(block, t).wait_send()
            return carry

        lax.fori_loop(0, BLOCKS, left, 0)


def per_device(query, keys, values, doc_lengths, w_out):
    rows, width = query.shape
    heads = width // HD
    part = rows // 2
    out_cols = w_out.shape[1] // lax.axis_size("head")
    dma = pltpu.SemaphoreType.DMA
    pairs = BLOCKS * (BLOCKS + 1) // 2
    flops = pairs * part * rows * 4 * HD + 2 * rows * w_out.shape[1] * width
    return pl.pallas_call(
        kernel,
        out_shape=jax.ShapeDtypeStruct((rows, out_cols), jnp.bfloat16),
        in_specs=[pl.BlockSpec(memory_space=pltpu.SMEM)] + [pl.BlockSpec(memory_space=pl.ANY)] * 4,
        out_specs=pl.BlockSpec(memory_space=pltpu.VMEM),
        scratch_shapes=[
            pltpu.VMEM((BLOCKS, part, HD), jnp.bfloat16),
            pltpu.VMEM((BLOCKS, 2, rows, HD), jnp.bfloat16),
            pltpu.VMEM((BLOCKS, part, 2 * HD), jnp.bfloat16),
            pltpu.VMEM((BLOCKS, 2 * HD, rows), jnp.bfloat16),
            pltpu.VMEM((BLOCKS, part, HD), jnp.float32),
            pltpu.VMEM((BLOCKS, part, 2 * HD), jnp.float32),
            [pltpu.VMEM((part // 2, rows), jnp.float32)] * 4,
            [pltpu.VMEM((part // 2, rows), jnp.bfloat16)] * 4,
            pltpu.VMEM((BLOCKS, part, HD), jnp.bfloat16),
            pltpu.VMEM((RING, rows, 2 * width), jnp.bfloat16),
            pltpu.VMEM((RING, 2, 2, width // 2, out_cols), jnp.bfloat16),
            pltpu.VMEM((part, out_cols), jnp.float32),
            dma((RING, 2, 3)),
            dma((BLOCKS,)),
            dma((BLOCKS,)),
            dma((BLOCKS,)),
            dma((BLOCKS,)),
            dma((2, BLOCKS)),
            dma((2, 2 * heads)),
            dma((RING, 2)),
            dma((RING, 2)),
            dma((RING,)),
            dma((RING,)),
            dma((2, 2, 2 * heads)),
            dma((2, 2, 2 * heads)),
            dma((2, 2, 2 * heads)),
            dma((2, 2, 2 * heads)),
            dma((2, RING, 2 * heads)),
            dma((2, RING)),
        ],
        compiler_params=pltpu.CompilerParams(
            collective_id=0, has_side_effects=True, vmem_limit_bytes=56 * 1024 * 1024
        ),
        cost_estimate=pl.CostEstimate(
            flops=flops, bytes_accessed=16 * 1024 * 1024, transcendentals=pairs * part * rows
        ),
    )(doc_lengths, query, keys, values, w_out.reshape(2, width // 2, w_out.shape[1]))


def solution(mesh):
    return jax.shard_map(
        per_device,
        mesh=mesh,
        in_specs=(P("ctx", "head"), P("ctx", "head"), P("ctx", "head"), P(), P("head", None)),
        out_specs=P("ctx", "head"),
        check_vma=False,
    )
```

```python
import functools
import math

import jax
import jax.numpy as jnp
from jax import lax
from jax.experimental import pallas as pl
from jax.experimental.pallas import tpu as pltpu
from jax.sharding import PartitionSpec as P

HD = 128
BLOCKS = 8
RING = 4
OTHER_DOC = -(2.0**20)
FLOOR = -5e5
MESH = pl.DeviceIdType.MESH


def kernel(
    lengths_ref, q_ref, k_ref, v_ref, w_ref, out_ref,
    q_in, kv_in, q_two, keys_across, top, accum, scores, shares, mixed, gathered, weights, total,
    send_sem, q_sem, kv_sem, share_send, share_sem, mixed_send, mixed_sem,
    w_send, w_sem, across_send, across_sem, ring_send, ring_sem, relay_send, relay_sem, pair_send, pair_sem,
):
    rows = q_ref.shape[0]
    part = rows // 2
    heads = q_ref.shape[1] // HD
    width = heads * HD
    out_cols = out_ref.shape[1]
    ctx, head = lax.axis_index("ctx"), lax.axis_index("head")
    half, place = ctx // BLOCKS, lax.rem(ctx, BLOCKS)
    place_x, place_y = place // RING, lax.rem(place, RING)
    z, core = head // 2, lax.rem(head, 2)
    other = 1 - core
    first = half * BLOCKS
    sibling = (ctx, z * 2 + other)
    z_up, z_down, z_far = lax.rem(z + 1, RING), lax.rem(z + 3, RING), lax.rem(z + 2, RING)
    works = place_y < heads
    partner = ((RING - 1 - ctx // RING) * RING + place_y, head)

    barrier = pltpu.get_barrier_semaphore()
    for block in range(BLOCKS):
        for c in range(2):
            @pl.when((block != place) | (c != core))
            def _():
                pl.semaphore_signal(
                    barrier, inc=1, device_id=(first + block, z * 2 + c), device_id_type=MESH
                )
    for away in range(1, RING):
        for c in range(2):
            pl.semaphore_signal(
                barrier, inc=1, device_id=(ctx, lax.rem(z + away, RING) * 2 + c), device_id_type=MESH
            )
    pl.semaphore_signal(barrier, inc=1, device_id=partner, device_id_type=MESH)
    pl.semaphore_wait(barrier, 2 * BLOCKS - 1 + 2 * (RING - 1) + 1)

    def outgoing(away, c, n):
        local = lax.rem(place_y + away, RING)
        target = core * RING + local
        cols = pl.ds(pl.multiple_of(local * HD, HD), HD)
        span = pl.ds(c * part, part)
        source, dest, sem = (
            (k_ref, kv_in.at[place, 0, span], kv_sem.at[place]),
            (v_ref, kv_in.at[place, 1, span], kv_sem.at[place]),
            (q_ref, q_in.at[place], q_sem.at[place]),
        )[n]
        here = target == place

        def remote():
            return pltpu.make_async_remote_copy(
                src_ref=source.at[span, cols], dst_ref=dest, send_sem=send_sem.at[away, c, n], recv_sem=sem,
                device_id=(first + target, z * 2 + c), device_id_type=MESH,
            )

        def start():
            if away == 0:
                @pl.when((local < heads) & here & (core == c))
                def _():
                    pltpu.make_async_copy(source.at[span, cols], dest, sem).start()

                @pl.when((local < heads) & jnp.logical_not(here & (core == c)))
                def _():
                    remote().start()
            else:
                @pl.when(local < heads)
                def _():
                    remote().start()

        def finish():
            sent = local < heads
            if away == 0:
                sent &= jnp.logical_not(here & (core == c))

            @pl.when(sent)
            def _():
                remote().wait_send()

        return start, finish

    def weight_cols(target):
        return pl.ds(pl.multiple_of(target * out_cols, 128), out_cols)

    def weight_copy(away, c):
        target = lax.rem(z + away, RING) * 2 + c
        return pltpu.make_async_remote_copy(
            src_ref=w_ref.at[half, :, weight_cols(target)], dst_ref=weights.at[z, core, half],
            send_sem=w_send.at[away, c], recv_sem=w_sem.at[z, core],
            device_id=(ctx, target), device_id_type=MESH,
        )

    def weight_pair():
        return pltpu.make_async_remote_copy(
            src_ref=w_ref.at[:, :, weight_cols(z * 2 + other)], dst_ref=weights.at[z, core],
            send_sem=w_send.at[0, 0], recv_sem=w_sem.at[z, core],
            device_id=sibling, device_id_type=MESH,
        )

    def weight_across(away):
        piece = weights.at[lax.rem(z + away, RING), :, half]
        return pltpu.make_async_remote_copy(
            src_ref=piece, dst_ref=piece, send_sem=across_send.at[away], recv_sem=across_sem.at[away],
            device_id=partner, device_id_type=MESH,
        )

    def hand_across(away):
        source = lax.rem(z + away, RING)
        for c in range(2):
            piece = weights.at[source, c, half]
            pltpu.make_async_copy(piece, piece, w_sem.at[source, c]).wait()
        weight_across(away).start()

    def weights_here(away):
        source = lax.rem(z + away, RING)
        if away == 0:
            for c in range(2):
                piece = weights.at[source, c]
                pltpu.make_async_copy(piece, piece, w_sem.at[source, c]).wait()
        else:
            piece = weights.at[source, :, 1 - half]
            pltpu.make_async_copy(piece, piece, across_sem.at[away]).wait()

    sends = [[outgoing(away, c, n) for away in (1, 3, 2, 0) for c in range(2)] for n in range(3)]
    for group, away in zip(sends, (2, 1, 3)):
        for start, _ in group:
            start()
        for c in range(2):
            weight_copy(away, c).start()
    weight_pair().start()
    pltpu.make_async_copy(w_ref.at[:, :, weight_cols(head)], weights.at[z, core], w_sem.at[z, core]).start()

    scale = math.log2(math.e) / math.sqrt(HD)
    hh = heads * place_x + place_y

    def share(block):
        span = pl.ds(pl.multiple_of(core * part, 128), part)
        return pltpu.make_async_remote_copy(
            src_ref=kv_in.at[block, :, span], dst_ref=kv_in.at[block, :, span],
            send_sem=share_send.at[block], recv_sem=share_sem.at[block],
            device_id=sibling, device_id_type=MESH,
        )

    def shared(block):
        span = pl.ds(pl.multiple_of(other * part, 128), part)
        return pltpu.make_async_copy(
            kv_in.at[block, :, span], kv_in.at[block, :, span], share_sem.at[block]
        )

    tile, group = part // 2, 16
    chunks = rows // HD

    def half_rows(c, t):
        return pl.ds(pl.multiple_of(c * part + t * tile, 128), tile)

    def mixed_target(t):
        return gathered.at[z, half_rows(core, t), pl.ds(pl.multiple_of(hh * HD, HD), HD)]

    def mixed_source(block, t):
        return mixed.at[block, pl.ds(pl.multiple_of(t * tile, 128), tile)]

    def mixed_copy(block, t):
        return pltpu.make_async_remote_copy(
            src_ref=mixed_source(block, t), dst_ref=mixed_target(t),
            send_sem=mixed_send.at[t, block], recv_sem=mixed_sem.at[t, hh],
            device_id=(first + block, head), device_id_type=MESH,
        )

    def finish(block, t):
        result = accum[block, pl.ds(pl.multiple_of(t * tile, 128), tile)]
        mixed[block, pl.ds(pl.multiple_of(t * tile, 128), tile)] = (
            result[:, :HD] / result[:, HD:]
        ).astype(jnp.bfloat16)

        @pl.when(block == place)
        def _():
            pltpu.make_async_copy(mixed_source(block, t), mixed_target(t), mixed_sem.at[t, hh]).start()

        @pl.when(block != place)
        def _():
            mixed_copy(block, t).start()

    def attend(tiles, t):
        first_row = pl.multiple_of(t * tile, 128)

        def score(n):
            q_block, k_block, _ = tiles[n]
            scores[n][...] = jnp.dot(
                q_two[q_block, pl.ds(first_row, tile)], keys_across[k_block], preferred_element_type=jnp.float32
            )

        def soften(n):
            q_block, _, diagonal = tiles[n]
            rows_here = pl.ds(first_row, tile)
            old = top[q_block, rows_here]
            news = []
            for g in range(tile // group):
                piece = scores[n][pl.ds(g * group, group)]
                parts = [piece[:, m * HD : (m + 1) * HD] for m in range(chunks)]
                if diagonal:
                    row = core * part + first_row + g * group
                    row = lax.broadcasted_iota(jnp.int32, (group, HD), 0) + row
                    lanes = lax.broadcasted_iota(jnp.int32, (group, HD), 1)
                    parts = [jnp.where(lanes + m * HD <= row, one, OTHER_DOC) for m, one in enumerate(parts)]
                most = functools.reduce(jnp.maximum, parts)
                new = jnp.maximum(old[g * group : (g + 1) * group], jnp.max(most, axis=1, keepdims=True))
                news.append(new)
                weight = [jnp.exp2((one - new) * scale).astype(jnp.bfloat16) for one in parts]
                shares[n][pl.ds(g * group, group)] = jnp.concatenate(weight, axis=1)
            new = jnp.concatenate(news, axis=0)
            top[q_block, rows_here] = new
            return jnp.exp2((old - new) * scale)

        def mix(n, factor):
            q_block, k_block, _ = tiles[n]
            rows_here = pl.ds(first_row, tile)
            values = kv_in[k_block, 1]
            values = jnp.concatenate([values, jnp.ones_like(values)], axis=1)
            product = jnp.dot(shares[n][...], values, preferred_element_type=jnp.float32)
            factor = jnp.concatenate([factor, factor], axis=1)
            accum[q_block, rows_here] = accum[q_block, rows_here] * factor + product

        score(0)
        for n in range(len(tiles)):
            if n + 1 < len(tiles):
                score(n + 1)
            mix(n, soften(n))

    order = [(dx, dy) for dy in (2, 1, 3, 0) for dx in (1, 0)]

    def each(action, t):
        for dx, dy in order:
            row, local = lax.rem(place_x + dx, 2), lax.rem(place_y + dy, RING)

            @pl.when(local < heads)
            def _():
                action(heads * row + local, t)

    mine = [half_rows(core, t) for t in range(2)]
    theirs = [half_rows(other, t) for t in range(2)]
    far_rows = [
        [pl.ds(pl.multiple_of(core * part + t * tile + n * (tile // 2), 128), tile // 2) for n in range(2)]
        for t in range(2)
    ]

    def piece_of(source, span, piece):
        return gathered.at[source, span, pl.ds(pl.multiple_of(piece * HD, HD), HD)]

    def ring(source, span, piece, target, send, recv):
        return pltpu.make_async_remote_copy(
            src_ref=piece_of(source, span, piece), dst_ref=piece_of(source, span, piece),
            send_sem=send.at[piece], recv_sem=recv.at[piece],
            device_id=(ctx, target * 2 + core), device_id_type=MESH,
        )

    def to_pair(source, piece, t):
        return pltpu.make_async_remote_copy(
            src_ref=piece_of(source, mine[t], piece), dst_ref=piece_of(source, mine[t], piece),
            send_sem=pair_send.at[t, source, piece], recv_sem=pair_sem.at[t, source],
            device_id=sibling, device_id_type=MESH,
        )

    def piece_landed(source, span, piece, sem):
        here = piece_of(source, span, piece)
        pltpu.make_async_copy(here, here, sem.at[piece]).wait()

    def up(piece, t):
        return ring(z, mine[t], piece, z_up, ring_send.at[t, 0], ring_sem.at[t, 0])

    def down(piece, t):
        return ring(z, mine[t], piece, z_down, ring_send.at[t, 1], ring_sem.at[t, 1])

    def relay_up(piece, t):
        return ring(z_down, far_rows[t][0], piece, z_up, relay_send.at[t, 0], relay_sem.at[t, 0])

    def relay_down(piece, t):
        return ring(z_up, far_rows[t][1], piece, z_down, relay_send.at[t, 1], relay_sem.at[t, 1])

    def send_own(piece, t):
        piece_landed(z, mine[t], piece, mixed_sem.at[t])
        up(piece, t).start()
        down(piece, t).start()
        to_pair(z, piece, t).start()

    def pass_on(piece, t):
        piece_landed(z_down, mine[t], piece, ring_sem.at[t, 0])
        relay_up(piece, t).start()
        to_pair(z_down, piece, t).start()
        piece_landed(z_up, mine[t], piece, ring_sem.at[t, 1])
        relay_down(piece, t).start()
        to_pair(z_up, piece, t).start()

    def take_far(piece, t):
        piece_landed(z_far, far_rows[t][0], piece, relay_sem.at[t, 0])
        piece_landed(z_far, far_rows[t][1], piece, relay_sem.at[t, 1])
        to_pair(z_far, piece, t).start()

    @pl.when(works)
    def _():
        def block_at(step):
            dx = jnp.where((step == 3) | (step == 4) | (step == 5) | (step == 7), 1, 0)
            dy = jnp.where(
                (step == 1) | (step == 4), 1, jnp.where((step == 2) | (step == 5), 3, jnp.where(step >= 6, 2, 0))
            )
            return lax.rem(place_x + dx, 2) * RING + lax.rem(place_y + dy, RING)

        def receive(step):
            block = block_at(step)
            span = pl.ds(pl.multiple_of(core * part, 128), part)
            arrived = kv_in.at[block, :, span]
            pltpu.make_async_copy(arrived, arrived, kv_sem.at[block]).wait()
            share(block).start()

        receive(0)

        def limits(shape, dim):
            index = lax.broadcasted_iota(jnp.int32, shape, dim)
            begin, end = jnp.zeros(shape, jnp.int32), jnp.zeros(shape, jnp.int32)
            last = jnp.int32(0)
            for n in range(lengths_ref.shape[0]):
                begin = jnp.where(index == n, last, begin)
                last = last + lengths_ref[n]
                end = jnp.where(index == n, last, end)
            return begin, end

        q_begin, q_end = limits((8, HD), 1)
        k_begin, k_end = limits((8, HD), 0)

        def blank(block, carry):
            start = (half * BLOCKS + block) * rows
            place_q = lax.broadcasted_iota(jnp.int32, (part // 8, 8, HD), 0) * 8
            place_q = place_q + lax.broadcasted_iota(jnp.int32, (part // 8, 8, HD), 1) + (start + core * part)
            same = (place_q >= q_begin[None]) & (place_q < q_end[None])
            lanes_q = jnp.where(same, 0.0, OTHER_DOC).reshape(part, HD)
            q_two[block, :, pl.ds(HD, HD)] = lanes_q.astype(jnp.bfloat16)
            for m in range(chunks):
                place_k = lax.broadcasted_iota(jnp.int32, (8, HD), 1) + (start + m * HD)
                same = (place_k >= k_begin) & (place_k < k_end)
                ones = jnp.where(same, 1.0, 0.0)
                ones = jnp.concatenate([ones, jnp.zeros((HD - 8, HD), jnp.float32)], axis=0)
                keys_across[block, pl.ds(HD, HD), pl.ds(m * HD, HD)] = ones.astype(jnp.bfloat16)
            top[block] = jnp.full((part, HD), FLOOR, jnp.float32)
            accum[block] = jnp.zeros((part, 2 * HD), jnp.float32)
            return carry

        lax.fori_loop(0, BLOCKS, blank, 0)

        ahead = BLOCKS - 2

        def take(turn, carry):
            t, step = turn // BLOCKS, lax.rem(turn, BLOCKS)
            for late, away in zip(range(BLOCKS - 3, BLOCKS), (1, 3, 2)):
                @pl.when(turn == late)
                def _():
                    hand_across(away)

            @pl.when(turn < ahead)
            def _():
                receive(turn + 1)

            @pl.when((turn > ahead) & (turn < BLOCKS))
            def _():
                receive(turn)

            block = jnp.where(t == 0, block_at(step), step)

            @pl.when(t == 0)
            def _():
                pltpu.make_async_copy(q_in.at[block], q_in.at[block], q_sem.at[block]).wait()
                q_two[block, :, pl.ds(0, HD)] = q_in[block]
                shared(block).wait()
                keys_across[block, pl.ds(0, HD)] = kv_in[block, 0].T

            def with_past(before):
                past = jnp.where(t == 0, block_at(before), before)
                return jnp.maximum(block, past), jnp.minimum(block, past), False

            def four_at_once(count, inner):
                attend([with_past(4 * count + n) for n in range(4)], t)
                return inner

            lax.fori_loop(0, step // 4, four_at_once, 0)
            for rest in range(4):
                @pl.when(lax.rem(step, 4) == rest)
                def _():
                    attend([with_past(step - 1 - n) for n in range(rest)] + [(block, block, True)], t)

            @pl.when(t == 1)
            def _():
                finish(block, 1)

            @pl.when(turn == BLOCKS - 1)
            def _():
                def finish_all(count, inner):
                    finish(block_at(BLOCKS - 1 - count), 0)
                    return inner

                lax.fori_loop(0, BLOCKS, finish_all, 0)

            for when, action in ((BLOCKS + 5, send_own), (BLOCKS + 6, pass_on), (BLOCKS + 7, take_far)):
                @pl.when(turn == when)
                def _():
                    each(action, 0)

            return carry

        lax.fori_loop(0, 2 * BLOCKS, take, 0)

    @pl.when(jnp.logical_not(works))
    def _():
        for away in (1, 3, 2):
            hand_across(away)
        for action in (send_own, pass_on, take_far):
            each(action, 0)

    def half_landed(away, t):
        source = lax.rem(z + away, RING)
        here = gathered.at[source, theirs[t]]
        pltpu.make_async_copy(here, here, pair_sem.at[t, source]).wait()

    def project(aways, t, start, last):
        def some_rows(c, carry):
            span = half_rows(c, t)
            product = None if start else total[pl.ds(pl.multiple_of(c * tile, 128), tile)]
            for away in aways:
                source = lax.rem(z + away, RING)
                term = jnp.dot(
                    gathered[source, span], weights[source].reshape(2 * width, out_cols),
                    preferred_element_type=jnp.float32,
                )
                product = term if product is None else product + term
            if last:
                out_ref[span] = product.astype(jnp.bfloat16)
            else:
                total[pl.ds(pl.multiple_of(c * tile, 128), tile)] = product
            return carry

        lax.fori_loop(0, 2, some_rows, 0)

    each(send_own, 1)
    for away in range(RING):
        half_landed(away, 0)
        weights_here(away)
    project((0, 1, 2, 3), 0, True, True)
    each(pass_on, 1)
    for away in (0, 1, 3):
        half_landed(away, 1)
    project((0, 1, 3), 1, True, False)
    each(take_far, 1)
    half_landed(2, 1)
    project((2,), 1, False, True)

    def all_left(piece, t):
        for copy in (up, down, relay_up, relay_down):
            copy(piece, t).wait_send()
        for source in range(RING):
            to_pair(source, piece, t).wait_send()

    for t in range(2):
        each(all_left, t)
    for away in (2, 1, 3):
        for c in range(2):
            weight_copy(away, c).wait_send()
        weight_across(away).wait_send()
    weight_pair().wait_send()
    for group in sends:
        for _, finish in group:
            finish()

    @pl.when(works)
    def _():
        def left(block, carry):
            share(block).wait_send()

            @pl.when(block != place)
            def _():
                for t in range(2):
                    mixed_copy(block, t).wait_send()
            return carry

        lax.fori_loop(0, BLOCKS, left, 0)


def per_device(query, keys, values, doc_lengths, w_out):
    rows, width = query.shape
    heads = width // HD
    part = rows // 2
    out_cols = w_out.shape[1] // lax.axis_size("head")
    dma = pltpu.SemaphoreType.DMA
    pairs = BLOCKS * (BLOCKS + 1) // 2
    flops = pairs * part * rows * 4 * HD + 2 * rows * w_out.shape[1] * width
    return pl.pallas_call(
        kernel,
        out_shape=jax.ShapeDtypeStruct((rows, out_cols), jnp.bfloat16),
        in_specs=[pl.BlockSpec(memory_space=pltpu.SMEM)] + [pl.BlockSpec(memory_space=pl.ANY)] * 4,
        out_specs=pl.BlockSpec(memory_space=pltpu.VMEM),
        scratch_shapes=[
            pltpu.VMEM((BLOCKS, part, HD), jnp.bfloat16),
            pltpu.VMEM((BLOCKS, 2, rows, HD), jnp.bfloat16),
            pltpu.VMEM((BLOCKS, part, 2 * HD), jnp.bfloat16),
            pltpu.VMEM((BLOCKS, 2 * HD, rows), jnp.bfloat16),
            pltpu.VMEM((BLOCKS, part, HD), jnp.float32),
            pltpu.VMEM((BLOCKS, part, 2 * HD), jnp.float32),
            [pltpu.VMEM((part // 2, rows), jnp.float32)] * 4,
            [pltpu.VMEM((part // 2, rows), jnp.bfloat16)] * 4,
            pltpu.VMEM((BLOCKS, part, HD), jnp.bfloat16),
            pltpu.VMEM((RING, rows, 2 * width), jnp.bfloat16),
            pltpu.VMEM((RING, 2, 2, width // 2, out_cols), jnp.bfloat16),
            pltpu.VMEM((part, out_cols), jnp.float32),
            dma((RING, 2, 3)),
            dma((BLOCKS,)),
            dma((BLOCKS,)),
            dma((BLOCKS,)),
            dma((BLOCKS,)),
            dma((2, BLOCKS)),
            dma((2, 2 * heads)),
            dma((RING, 2)),
            dma((RING, 2)),
            dma((RING,)),
            dma((RING,)),
            dma((2, 2, 2 * heads)),
            dma((2, 2, 2 * heads)),
            dma((2, 2, 2 * heads)),
            dma((2, 2, 2 * heads)),
            dma((2, RING, 2 * heads)),
            dma((2, RING)),
        ],
        compiler_params=pltpu.CompilerParams(
            collective_id=0, has_side_effects=True, vmem_limit_bytes=56 * 1024 * 1024
        ),
        cost_estimate=pl.CostEstimate(
            flops=flops, bytes_accessed=16 * 1024 * 1024, transcendentals=pairs * part * rows
        ),
    )(doc_lengths, query, keys, values, w_out.reshape(2, width // 2, w_out.shape[1]))


def solution(mesh):
    return jax.shard_map(
        per_device,
        mesh=mesh,
        in_specs=(P("ctx", "head"), P("ctx", "head"), P("ctx", "head"), P(), P("head", None)),
        out_specs=P("ctx", "head"),
        check_vma=False,
    )
```

```python
import functools
import math

import jax
import jax.numpy as jnp
from jax import lax
from jax.experimental import pallas as pl
from jax.experimental.pallas import tpu as pltpu
from jax.sharding import PartitionSpec as P

HD = 128
BLOCKS = 8
RING = 4
OTHER_DOC = -(2.0**20)
FLOOR = -5e5
MESH = pl.DeviceIdType.MESH


def kernel(
    lengths_ref, q_ref, k_ref, v_ref, w_ref, out_ref,
    q_in, kv_in, q_two, keys_across, top, accum, scores, shares, mixed, gathered, weights, total,
    send_sem, q_sem, kv_sem, share_send, share_sem, mixed_send, mixed_sem,
    w_send, w_sem, across_send, across_sem, ring_send, ring_sem, relay_send, relay_sem, pair_send, pair_sem,
):
    rows = q_ref.shape[0]
    part = rows // 2
    heads = q_ref.shape[1] // HD
    width = heads * HD
    out_cols = out_ref.shape[1]
    ctx, head = lax.axis_index("ctx"), lax.axis_index("head")
    half, place = ctx // BLOCKS, lax.rem(ctx, BLOCKS)
    place_x, place_y = place // RING, lax.rem(place, RING)
    z, core = head // 2, lax.rem(head, 2)
    other = 1 - core
    first = half * BLOCKS
    sibling = (ctx, z * 2 + other)
    z_up, z_down, z_far = lax.rem(z + 1, RING), lax.rem(z + 3, RING), lax.rem(z + 2, RING)
    works = place_y < heads
    partner = ((RING - 1 - ctx // RING) * RING + place_y, head)

    barrier = pltpu.get_barrier_semaphore()
    for block in range(BLOCKS):
        for c in range(2):
            @pl.when((block != place) | (c != core))
            def _():
                pl.semaphore_signal(
                    barrier, inc=1, device_id=(first + block, z * 2 + c), device_id_type=MESH
                )
    for away in range(1, RING):
        for c in range(2):
            pl.semaphore_signal(
                barrier, inc=1, device_id=(ctx, lax.rem(z + away, RING) * 2 + c), device_id_type=MESH
            )
    pl.semaphore_signal(barrier, inc=1, device_id=partner, device_id_type=MESH)
    pl.semaphore_wait(barrier, 2 * BLOCKS - 1 + 2 * (RING - 1) + 1)

    def outgoing(away, c, n):
        local = lax.rem(place_y + away, RING)
        target = core * RING + local
        cols = pl.ds(pl.multiple_of(local * HD, HD), HD)
        span = pl.ds(c * part, part)
        source, dest, sem = (
            (k_ref, kv_in.at[place, 0, span], kv_sem.at[place]),
            (v_ref, kv_in.at[place, 1, span], kv_sem.at[place]),
            (q_ref, q_in.at[place], q_sem.at[place]),
        )[n]
        here = target == place

        def remote():
            return pltpu.make_async_remote_copy(
                src_ref=source.at[span, cols], dst_ref=dest, send_sem=send_sem.at[away, c, n], recv_sem=sem,
                device_id=(first + target, z * 2 + c), device_id_type=MESH,
            )

        def start():
            if away == 0:
                @pl.when((local < heads) & here & (core == c))
                def _():
                    pltpu.make_async_copy(source.at[span, cols], dest, sem).start()

                @pl.when((local < heads) & jnp.logical_not(here & (core == c)))
                def _():
                    remote().start()
            else:
                @pl.when(local < heads)
                def _():
                    remote().start()

        def finish():
            sent = local < heads
            if away == 0:
                sent &= jnp.logical_not(here & (core == c))

            @pl.when(sent)
            def _():
                remote().wait_send()

        return start, finish

    def weight_cols(target):
        return pl.ds(pl.multiple_of(target * out_cols, 128), out_cols)

    def weight_copy(away, c):
        target = lax.rem(z + away, RING) * 2 + c
        return pltpu.make_async_remote_copy(
            src_ref=w_ref.at[half, :, weight_cols(target)], dst_ref=weights.at[z, core, half],
            send_sem=w_send.at[away, c], recv_sem=w_sem.at[z, core],
            device_id=(ctx, target), device_id_type=MESH,
        )

    def weight_pair():
        return pltpu.make_async_remote_copy(
            src_ref=w_ref.at[:, :, weight_cols(z * 2 + other)], dst_ref=weights.at[z, core],
            send_sem=w_send.at[0, 0], recv_sem=w_sem.at[z, core],
            device_id=sibling, device_id_type=MESH,
        )

    def weight_across(away):
        piece = weights.at[lax.rem(z + away, RING), :, half]
        return pltpu.make_async_remote_copy(
            src_ref=piece, dst_ref=piece, send_sem=across_send.at[away], recv_sem=across_sem.at[away],
            device_id=partner, device_id_type=MESH,
        )

    def hand_across(away):
        source = lax.rem(z + away, RING)
        for c in range(2):
            piece = weights.at[source, c, half]
            pltpu.make_async_copy(piece, piece, w_sem.at[source, c]).wait()
        weight_across(away).start()

    def weights_here(away):
        source = lax.rem(z + away, RING)
        if away == 0:
            for c in range(2):
                piece = weights.at[source, c]
                pltpu.make_async_copy(piece, piece, w_sem.at[source, c]).wait()
        else:
            piece = weights.at[source, :, 1 - half]
            pltpu.make_async_copy(piece, piece, across_sem.at[away]).wait()

    sends = [[outgoing(away, c, n) for away in (1, 3, 2, 0) for c in range(2)] for n in range(3)]
    for group, away in zip(sends, (2, 1, 3)):
        for start, _ in group:
            start()
        for c in range(2):
            weight_copy(away, c).start()
    weight_pair().start()
    pltpu.make_async_copy(w_ref.at[:, :, weight_cols(head)], weights.at[z, core], w_sem.at[z, core]).start()

    scale = math.log2(math.e) / math.sqrt(HD)
    hh = heads * place_x + place_y

    def share(block):
        span = pl.ds(pl.multiple_of(core * part, 128), part)
        return pltpu.make_async_remote_copy(
            src_ref=kv_in.at[block, :, span], dst_ref=kv_in.at[block, :, span],
            send_sem=share_send.at[block], recv_sem=share_sem.at[block],
            device_id=sibling, device_id_type=MESH,
        )

    def shared(block):
        span = pl.ds(pl.multiple_of(other * part, 128), part)
        return pltpu.make_async_copy(
            kv_in.at[block, :, span], kv_in.at[block, :, span], share_sem.at[block]
        )

    sizes, group = (part * 3 // 4, part // 4), 16
    offsets = (0, sizes[0])
    chunks = rows // HD

    def half_rows(c, t):
        return pl.ds(pl.multiple_of(c * part + offsets[t], 128), sizes[t])

    def mixed_target(t):
        return gathered.at[z, half_rows(core, t), pl.ds(pl.multiple_of(hh * HD, HD), HD)]

    def mixed_source(block, t):
        return mixed.at[block, pl.ds(offsets[t], sizes[t])]

    def mixed_copy(block, t):
        return pltpu.make_async_remote_copy(
            src_ref=mixed_source(block, t), dst_ref=mixed_target(t),
            send_sem=mixed_send.at[t, block], recv_sem=mixed_sem.at[t, hh],
            device_id=(first + block, head), device_id_type=MESH,
        )

    def finish(block, t):
        result = accum[block, pl.ds(offsets[t], sizes[t])]
        mixed[block, pl.ds(offsets[t], sizes[t])] = (
            result[:, :HD] / result[:, HD:]
        ).astype(jnp.bfloat16)

        @pl.when(block == place)
        def _():
            pltpu.make_async_copy(mixed_source(block, t), mixed_target(t), mixed_sem.at[t, hh]).start()

        @pl.when(block != place)
        def _():
            mixed_copy(block, t).start()

    def attend(tiles, t):
        first_row, tile = offsets[t], sizes[t]
        score_refs, share_refs = scores[2 * t :], shares[2 * t :]

        def score(n):
            q_block, k_block, _ = tiles[n]
            score_refs[n][...] = jnp.dot(
                q_two[q_block, pl.ds(first_row, tile)], keys_across[k_block], preferred_element_type=jnp.float32
            )

        def soften(n):
            q_block, _, diagonal = tiles[n]
            rows_here = pl.ds(first_row, tile)
            old = top[q_block, rows_here]
            news = []
            for g in range(tile // group):
                piece = score_refs[n][pl.ds(g * group, group)]
                parts = [piece[:, m * HD : (m + 1) * HD] for m in range(chunks)]
                if diagonal:
                    row = core * part + first_row + g * group
                    row = lax.broadcasted_iota(jnp.int32, (group, HD), 0) + row
                    lanes = lax.broadcasted_iota(jnp.int32, (group, HD), 1)
                    parts = [jnp.where(lanes + m * HD <= row, one, OTHER_DOC) for m, one in enumerate(parts)]
                most = functools.reduce(jnp.maximum, parts)
                new = jnp.maximum(old[g * group : (g + 1) * group], jnp.max(most, axis=1, keepdims=True))
                news.append(new)
                weight = [jnp.exp2((one - new) * scale).astype(jnp.bfloat16) for one in parts]
                share_refs[n][pl.ds(g * group, group)] = jnp.concatenate(weight, axis=1)
            new = jnp.concatenate(news, axis=0)
            top[q_block, rows_here] = new
            return jnp.exp2((old - new) * scale)

        def mix(n, factor):
            q_block, k_block, _ = tiles[n]
            rows_here = pl.ds(first_row, tile)
            values = kv_in[k_block, 1]
            values = jnp.concatenate([values, jnp.ones_like(values)], axis=1)
            product = jnp.dot(share_refs[n][...], values, preferred_element_type=jnp.float32)
            factor = jnp.concatenate([factor, factor], axis=1)
            accum[q_block, rows_here] = accum[q_block, rows_here] * factor + product

        score(0)
        for n in range(len(tiles)):
            if n + 1 < len(tiles):
                score(n + 1)
            mix(n, soften(n))

    order = [(dx, dy) for dy in (2, 1, 3, 0) for dx in (1, 0)]

    def each(action, t):
        for dx, dy in order:
            row, local = lax.rem(place_x + dx, 2), lax.rem(place_y + dy, RING)

            @pl.when(local < heads)
            def _():
                action(heads * row + local, t)

    mine = [half_rows(core, t) for t in range(2)]
    theirs = [half_rows(other, t) for t in range(2)]
    far_rows = [
        [
            pl.ds(pl.multiple_of(core * part + offsets[t] + n * (sizes[t] // 2), 64), sizes[t] // 2)
            for n in range(2)
        ]
        for t in range(2)
    ]

    def piece_of(source, span, piece):
        return gathered.at[source, span, pl.ds(pl.multiple_of(piece * HD, HD), HD)]

    def ring(source, span, piece, target, send, recv):
        return pltpu.make_async_remote_copy(
            src_ref=piece_of(source, span, piece), dst_ref=piece_of(source, span, piece),
            send_sem=send.at[piece], recv_sem=recv.at[piece],
            device_id=(ctx, target * 2 + core), device_id_type=MESH,
        )

    def to_pair(source, piece, t):
        return pltpu.make_async_remote_copy(
            src_ref=piece_of(source, mine[t], piece), dst_ref=piece_of(source, mine[t], piece),
            send_sem=pair_send.at[t, source, piece], recv_sem=pair_sem.at[t, source],
            device_id=sibling, device_id_type=MESH,
        )

    def piece_landed(source, span, piece, sem):
        here = piece_of(source, span, piece)
        pltpu.make_async_copy(here, here, sem.at[piece]).wait()

    def up(piece, t):
        return ring(z, mine[t], piece, z_up, ring_send.at[t, 0], ring_sem.at[t, 0])

    def down(piece, t):
        return ring(z, mine[t], piece, z_down, ring_send.at[t, 1], ring_sem.at[t, 1])

    def relay_up(piece, t):
        return ring(z_down, far_rows[t][0], piece, z_up, relay_send.at[t, 0], relay_sem.at[t, 0])

    def relay_down(piece, t):
        return ring(z_up, far_rows[t][1], piece, z_down, relay_send.at[t, 1], relay_sem.at[t, 1])

    def send_own(piece, t):
        piece_landed(z, mine[t], piece, mixed_sem.at[t])
        up(piece, t).start()
        down(piece, t).start()
        to_pair(z, piece, t).start()

    def pass_on(piece, t):
        piece_landed(z_down, mine[t], piece, ring_sem.at[t, 0])
        relay_up(piece, t).start()
        to_pair(z_down, piece, t).start()
        piece_landed(z_up, mine[t], piece, ring_sem.at[t, 1])
        relay_down(piece, t).start()
        to_pair(z_up, piece, t).start()

    def take_far(piece, t):
        piece_landed(z_far, far_rows[t][0], piece, relay_sem.at[t, 0])
        piece_landed(z_far, far_rows[t][1], piece, relay_sem.at[t, 1])
        to_pair(z_far, piece, t).start()

    @pl.when(works)
    def _():
        def block_at(step):
            dx = jnp.where((step == 3) | (step == 4) | (step == 5) | (step == 7), 1, 0)
            dy = jnp.where(
                (step == 1) | (step == 4), 1, jnp.where((step == 2) | (step == 5), 3, jnp.where(step >= 6, 2, 0))
            )
            return lax.rem(place_x + dx, 2) * RING + lax.rem(place_y + dy, RING)

        def receive(step):
            block = block_at(step)
            span = pl.ds(pl.multiple_of(core * part, 128), part)
            arrived = kv_in.at[block, :, span]
            pltpu.make_async_copy(arrived, arrived, kv_sem.at[block]).wait()
            share(block).start()

        receive(0)

        def limits(shape, dim):
            index = lax.broadcasted_iota(jnp.int32, shape, dim)
            begin, end = jnp.zeros(shape, jnp.int32), jnp.zeros(shape, jnp.int32)
            last = jnp.int32(0)
            for n in range(lengths_ref.shape[0]):
                begin = jnp.where(index == n, last, begin)
                last = last + lengths_ref[n]
                end = jnp.where(index == n, last, end)
            return begin, end

        q_begin, q_end = limits((8, HD), 1)
        k_begin, k_end = limits((8, HD), 0)

        def blank(block, carry):
            start = (half * BLOCKS + block) * rows
            place_q = lax.broadcasted_iota(jnp.int32, (part // 8, 8, HD), 0) * 8
            place_q = place_q + lax.broadcasted_iota(jnp.int32, (part // 8, 8, HD), 1) + (start + core * part)
            same = (place_q >= q_begin[None]) & (place_q < q_end[None])
            lanes_q = jnp.where(same, 0.0, OTHER_DOC).reshape(part, HD)
            q_two[block, :, pl.ds(HD, HD)] = lanes_q.astype(jnp.bfloat16)
            for m in range(chunks):
                place_k = lax.broadcasted_iota(jnp.int32, (8, HD), 1) + (start + m * HD)
                same = (place_k >= k_begin) & (place_k < k_end)
                ones = jnp.where(same, 1.0, 0.0)
                ones = jnp.concatenate([ones, jnp.zeros((HD - 8, HD), jnp.float32)], axis=0)
                keys_across[block, pl.ds(HD, HD), pl.ds(m * HD, HD)] = ones.astype(jnp.bfloat16)
            top[block] = jnp.full((part, HD), FLOOR, jnp.float32)
            accum[block] = jnp.zeros((part, 2 * HD), jnp.float32)
            return carry

        lax.fori_loop(0, BLOCKS, blank, 0)

        ahead = BLOCKS - 2

        def take(step, carry):
            for late, away in zip(range(BLOCKS - 3, BLOCKS), (1, 3, 2)):
                @pl.when(step == late)
                def _():
                    hand_across(away)

            @pl.when(step < ahead)
            def _():
                receive(step + 1)

            @pl.when(step > ahead)
            def _():
                receive(step)

            block = block_at(step)
            pltpu.make_async_copy(q_in.at[block], q_in.at[block], q_sem.at[block]).wait()
            q_two[block, :, pl.ds(0, HD)] = q_in[block]
            shared(block).wait()
            keys_across[block, pl.ds(0, HD)] = kv_in[block, 0].T

            def with_past(before):
                past = block_at(before)
                return jnp.maximum(block, past), jnp.minimum(block, past), False

            def two_at_once(count, inner):
                attend([with_past(2 * count + n) for n in range(2)], 0)
                return inner

            lax.fori_loop(0, step // 2, two_at_once, 0)
            for rest in range(2):
                @pl.when(lax.rem(step, 2) == rest)
                def _():
                    attend([with_past(step - 1 - n) for n in range(rest)] + [(block, block, True)], 0)

            return carry

        lax.fori_loop(0, BLOCKS, take, 0)

        def finish_all(count, carry):
            finish(block_at(BLOCKS - 1 - count), 0)
            return carry

        lax.fori_loop(0, BLOCKS, finish_all, 0)

        def take_rest(block, carry):
            def four_at_once(count, inner):
                attend([(block, 4 * count + n, False) for n in range(4)], 1)
                return inner

            lax.fori_loop(0, block // 4, four_at_once, 0)
            for rest in range(4):
                @pl.when(lax.rem(block, 4) == rest)
                def _():
                    attend([(block, block - 1 - n, False) for n in range(rest)] + [(block, block, True)], 1)

            finish(block, 1)

            for when, action in ((BLOCKS - 4, send_own), (BLOCKS - 2, pass_on)):
                @pl.when(block == when)
                def _():
                    each(action, 0)

            return carry

        lax.fori_loop(0, BLOCKS, take_rest, 0)

    @pl.when(jnp.logical_not(works))
    def _():
        for away in (1, 3, 2):
            hand_across(away)
        for action in (send_own, pass_on):
            each(action, 0)

    def half_landed(away, t):
        source = lax.rem(z + away, RING)
        here = gathered.at[source, theirs[t]]
        pltpu.make_async_copy(here, here, pair_sem.at[t, source]).wait()

    def project(aways, t, start, last):
        def some_rows(c, carry):
            span = half_rows(c, t)
            product = None if start else total[pl.ds(pl.multiple_of(c * sizes[t], 128), sizes[t])]
            for away in aways:
                source = lax.rem(z + away, RING)
                term = jnp.dot(
                    gathered[source, span], weights[source].reshape(2 * width, out_cols),
                    preferred_element_type=jnp.float32,
                )
                product = term if product is None else product + term
            if last:
                out_ref[span] = product.astype(jnp.bfloat16)
            else:
                total[pl.ds(pl.multiple_of(c * sizes[t], 128), sizes[t])] = product
            return carry

        lax.fori_loop(0, 2, some_rows, 0)

    each(send_own, 1)
    each(take_far, 0)
    for away in range(RING):
        half_landed(away, 0)
        weights_here(away)
    project((0, 1, 2, 3), 0, True, True)
    each(pass_on, 1)
    for away in (0, 1, 3):
        half_landed(away, 1)
    project((0, 1, 3), 1, True, False)
    each(take_far, 1)
    half_landed(2, 1)
    project((2,), 1, False, True)

    def all_left(piece, t):
        for copy in (up, down, relay_up, relay_down):
            copy(piece, t).wait_send()
        for source in range(RING):
            to_pair(source, piece, t).wait_send()

    for t in range(2):
        each(all_left, t)
    for away in (2, 1, 3):
        for c in range(2):
            weight_copy(away, c).wait_send()
        weight_across(away).wait_send()
    weight_pair().wait_send()
    for group in sends:
        for _, finish in group:
            finish()

    @pl.when(works)
    def _():
        def left(block, carry):
            share(block).wait_send()

            @pl.when(block != place)
            def _():
                for t in range(2):
                    mixed_copy(block, t).wait_send()
            return carry

        lax.fori_loop(0, BLOCKS, left, 0)


def per_device(query, keys, values, doc_lengths, w_out):
    rows, width = query.shape
    heads = width // HD
    part = rows // 2
    out_cols = w_out.shape[1] // lax.axis_size("head")
    dma = pltpu.SemaphoreType.DMA
    pairs = BLOCKS * (BLOCKS + 1) // 2
    sizes = [part * 3 // 4] * 2 + [part // 4] * 4
    flops = pairs * part * rows * 4 * HD + 2 * rows * w_out.shape[1] * width
    return pl.pallas_call(
        kernel,
        out_shape=jax.ShapeDtypeStruct((rows, out_cols), jnp.bfloat16),
        in_specs=[pl.BlockSpec(memory_space=pltpu.SMEM)] + [pl.BlockSpec(memory_space=pl.ANY)] * 4,
        out_specs=pl.BlockSpec(memory_space=pltpu.VMEM),
        scratch_shapes=[
            pltpu.VMEM((BLOCKS, part, HD), jnp.bfloat16),
            pltpu.VMEM((BLOCKS, 2, rows, HD), jnp.bfloat16),
            pltpu.VMEM((BLOCKS, part, 2 * HD), jnp.bfloat16),
            pltpu.VMEM((BLOCKS, 2 * HD, rows), jnp.bfloat16),
            pltpu.VMEM((BLOCKS, part, HD), jnp.float32),
            pltpu.VMEM((BLOCKS, part, 2 * HD), jnp.float32),
            [pltpu.VMEM((size, rows), jnp.float32) for size in sizes],
            [pltpu.VMEM((size, rows), jnp.bfloat16) for size in sizes],
            pltpu.VMEM((BLOCKS, part, HD), jnp.bfloat16),
            pltpu.VMEM((RING, rows, 2 * width), jnp.bfloat16),
            pltpu.VMEM((RING, 2, 2, width // 2, out_cols), jnp.bfloat16),
            pltpu.VMEM((part, out_cols), jnp.float32),
            dma((RING, 2, 3)),
            dma((BLOCKS,)),
            dma((BLOCKS,)),
            dma((BLOCKS,)),
            dma((BLOCKS,)),
            dma((2, BLOCKS)),
            dma((2, 2 * heads)),
            dma((RING, 2)),
            dma((RING, 2)),
            dma((RING,)),
            dma((RING,)),
            dma((2, 2, 2 * heads)),
            dma((2, 2, 2 * heads)),
            dma((2, 2, 2 * heads)),
            dma((2, 2, 2 * heads)),
            dma((2, RING, 2 * heads)),
            dma((2, RING)),
        ],
        compiler_params=pltpu.CompilerParams(
            collective_id=0, has_side_effects=True, vmem_limit_bytes=56 * 1024 * 1024
        ),
        cost_estimate=pl.CostEstimate(
            flops=flops, bytes_accessed=16 * 1024 * 1024, transcendentals=pairs * part * rows
        ),
    )(doc_lengths, query, keys, values, w_out.reshape(2, width // 2, w_out.shape[1]))


def solution(mesh):
    return jax.shard_map(
        per_device,
        mesh=mesh,
        in_specs=(P("ctx", "head"), P("ctx", "head"), P("ctx", "head"), P(), P("head", None)),
        out_specs=P("ctx", "head"),
        check_vma=False,
    )
```

```python
import functools
import math

import jax
import jax.numpy as jnp
from jax import lax
from jax.experimental import pallas as pl
from jax.experimental.pallas import tpu as pltpu
from jax.sharding import PartitionSpec as P

HD = 128
BLOCKS = 8
RING = 4
OTHER_DOC = -(2.0**20)
FLOOR = -5e5
MESH = pl.DeviceIdType.MESH


def kernel(
    lengths_ref, q_ref, k_ref, v_ref, w_ref, out_ref,
    q_in, kv_in, q_two, keys_across, top, accum, scores, shares, mixed, gathered, weights, total,
    send_sem, q_sem, kv_sem, share_send, share_sem, mixed_send, mixed_sem,
    w_send, w_sem, across_send, across_sem, ring_send, ring_sem, relay_send, relay_sem, pair_send, pair_sem,
):
    rows = q_ref.shape[0]
    part = rows // 2
    heads = q_ref.shape[1] // HD
    width = heads * HD
    out_cols = out_ref.shape[1]
    ctx, head = lax.axis_index("ctx"), lax.axis_index("head")
    half, place = ctx // BLOCKS, lax.rem(ctx, BLOCKS)
    place_x, place_y = place // RING, lax.rem(place, RING)
    z, core = head // 2, lax.rem(head, 2)
    other = 1 - core
    first = half * BLOCKS
    sibling = (ctx, z * 2 + other)
    z_up, z_down, z_far = lax.rem(z + 1, RING), lax.rem(z + 3, RING), lax.rem(z + 2, RING)
    works = place_y < heads
    partner = ((RING - 1 - ctx // RING) * RING + place_y, head)

    barrier = pltpu.get_barrier_semaphore()
    for block in range(BLOCKS):
        for c in range(2):
            @pl.when((block != place) | (c != core))
            def _():
                pl.semaphore_signal(
                    barrier, inc=1, device_id=(first + block, z * 2 + c), device_id_type=MESH
                )
    for away in range(1, RING):
        for c in range(2):
            pl.semaphore_signal(
                barrier, inc=1, device_id=(ctx, lax.rem(z + away, RING) * 2 + c), device_id_type=MESH
            )
    pl.semaphore_signal(barrier, inc=1, device_id=partner, device_id_type=MESH)
    pl.semaphore_wait(barrier, 2 * BLOCKS - 1 + 2 * (RING - 1) + 1)

    def outgoing(away, c, n):
        local = lax.rem(place_y + away, RING)
        target = core * RING + local
        cols = pl.ds(pl.multiple_of(local * HD, HD), HD)
        span = pl.ds(c * part, part)
        source, dest, sem = (
            (k_ref, kv_in.at[place, 0, span], kv_sem.at[place]),
            (v_ref, kv_in.at[place, 1, span], kv_sem.at[place]),
            (q_ref, q_in.at[place], q_sem.at[place]),
        )[n]
        here = target == place

        def remote():
            return pltpu.make_async_remote_copy(
                src_ref=source.at[span, cols], dst_ref=dest, send_sem=send_sem.at[away, c, n], recv_sem=sem,
                device_id=(first + target, z * 2 + c), device_id_type=MESH,
            )

        def start():
            if away == 0:
                @pl.when((local < heads) & here & (core == c))
                def _():
                    pltpu.make_async_copy(source.at[span, cols], dest, sem).start()

                @pl.when((local < heads) & jnp.logical_not(here & (core == c)))
                def _():
                    remote().start()
            else:
                @pl.when(local < heads)
                def _():
                    remote().start()

        def finish():
            sent = local < heads
            if away == 0:
                sent &= jnp.logical_not(here & (core == c))

            @pl.when(sent)
            def _():
                remote().wait_send()

        return start, finish

    def weight_cols(target):
        return pl.ds(pl.multiple_of(target * out_cols, 128), out_cols)

    def weight_copy(away, c):
        target = lax.rem(z + away, RING) * 2 + c
        return pltpu.make_async_remote_copy(
            src_ref=w_ref.at[half, :, weight_cols(target)], dst_ref=weights.at[z, core, half],
            send_sem=w_send.at[away, c], recv_sem=w_sem.at[z, core],
            device_id=(ctx, target), device_id_type=MESH,
        )

    def weight_pair():
        return pltpu.make_async_remote_copy(
            src_ref=w_ref.at[:, :, weight_cols(z * 2 + other)], dst_ref=weights.at[z, core],
            send_sem=w_send.at[0, 0], recv_sem=w_sem.at[z, core],
            device_id=sibling, device_id_type=MESH,
        )

    def weight_across(away):
        piece = weights.at[lax.rem(z + away, RING), :, half]
        return pltpu.make_async_remote_copy(
            src_ref=piece, dst_ref=piece, send_sem=across_send.at[away], recv_sem=across_sem.at[away],
            device_id=partner, device_id_type=MESH,
        )

    def hand_across(away):
        source = lax.rem(z + away, RING)
        for c in range(2):
            piece = weights.at[source, c, half]
            pltpu.make_async_copy(piece, piece, w_sem.at[source, c]).wait()
        weight_across(away).start()

    def weights_here(away):
        source = lax.rem(z + away, RING)
        if away == 0:
            for c in range(2):
                piece = weights.at[source, c]
                pltpu.make_async_copy(piece, piece, w_sem.at[source, c]).wait()
        else:
            piece = weights.at[source, :, 1 - half]
            pltpu.make_async_copy(piece, piece, across_sem.at[away]).wait()

    sends = [[outgoing(away, c, n) for away in (1, 3, 2, 0) for c in range(2)] for n in range(3)]
    for group, away in zip(sends, (2, 1, 3)):
        for start, _ in group:
            start()
        for c in range(2):
            weight_copy(away, c).start()
    weight_pair().start()
    pltpu.make_async_copy(w_ref.at[:, :, weight_cols(head)], weights.at[z, core], w_sem.at[z, core]).start()

    scale = math.log2(math.e) / math.sqrt(HD)
    hh = heads * place_x + place_y

    def share(block):
        span = pl.ds(pl.multiple_of(core * part, 128), part)
        return pltpu.make_async_remote_copy(
            src_ref=kv_in.at[block, :, span], dst_ref=kv_in.at[block, :, span],
            send_sem=share_send.at[block], recv_sem=share_sem.at[block],
            device_id=sibling, device_id_type=MESH,
        )

    def shared(block):
        span = pl.ds(pl.multiple_of(other * part, 128), part)
        return pltpu.make_async_copy(
            kv_in.at[block, :, span], kv_in.at[block, :, span], share_sem.at[block]
        )

    tile, group = part // 2, 16
    chunks = rows // HD

    def half_rows(c, t):
        return pl.ds(pl.multiple_of(c * part + t * tile, 128), tile)

    def mixed_target(t):
        return gathered.at[z, half_rows(core, t), pl.ds(pl.multiple_of(hh * HD, HD), HD)]

    def mixed_source(block, t):
        return mixed.at[block, pl.ds(pl.multiple_of(t * tile, 128), tile)]

    def mixed_copy(block, t):
        return pltpu.make_async_remote_copy(
            src_ref=mixed_source(block, t), dst_ref=mixed_target(t),
            send_sem=mixed_send.at[t, block], recv_sem=mixed_sem.at[t, hh],
            device_id=(first + block, head), device_id_type=MESH,
        )

    def finish(block, t):
        result = accum[block, pl.ds(pl.multiple_of(t * tile, 128), tile)]
        mixed[block, pl.ds(pl.multiple_of(t * tile, 128), tile)] = (
            result[:, :HD] / result[:, HD:]
        ).astype(jnp.bfloat16)

        @pl.when(block == place)
        def _():
            pltpu.make_async_copy(mixed_source(block, t), mixed_target(t), mixed_sem.at[t, hh]).start()

        @pl.when(block != place)
        def _():
            mixed_copy(block, t).start()

    def score(slot, q_block, k_block, t):
        scores[slot][...] = jnp.dot(
            q_two[q_block, pl.ds(pl.multiple_of(t * tile, 128), tile)], keys_across[k_block],
            preferred_element_type=jnp.float32,
        )

    def attend(tiles, t, following):
        first_row = pl.multiple_of(t * tile, 128)

        def soften(n):
            q_block, _, diagonal = tiles[n]
            rows_here = pl.ds(first_row, tile)
            old = top[q_block, rows_here]
            news = []
            for g in range(tile // group):
                piece = scores[n][pl.ds(g * group, group)]
                parts = [piece[:, m * HD : (m + 1) * HD] for m in range(chunks)]
                if diagonal:
                    row = core * part + first_row + g * group
                    row = lax.broadcasted_iota(jnp.int32, (group, HD), 0) + row
                    lanes = lax.broadcasted_iota(jnp.int32, (group, HD), 1)
                    parts = [jnp.where(lanes + m * HD <= row, one, OTHER_DOC) for m, one in enumerate(parts)]
                most = functools.reduce(jnp.maximum, parts)
                new = jnp.maximum(old[g * group : (g + 1) * group], jnp.max(most, axis=1, keepdims=True))
                news.append(new)
                weight = [jnp.exp2((one - new) * scale).astype(jnp.bfloat16) for one in parts]
                shares[n][pl.ds(g * group, group)] = jnp.concatenate(weight, axis=1)
            new = jnp.concatenate(news, axis=0)
            top[q_block, rows_here] = new
            return jnp.exp2((old - new) * scale)

        def mix(n, factor):
            q_block, k_block, _ = tiles[n]
            rows_here = pl.ds(first_row, tile)
            values = kv_in[k_block, 1]
            values = jnp.concatenate([values, jnp.ones_like(values)], axis=1)
            product = jnp.dot(shares[n][...], values, preferred_element_type=jnp.float32)
            factor = jnp.concatenate([factor, factor], axis=1)
            accum[q_block, rows_here] = accum[q_block, rows_here] * factor + product

        for n in range(len(tiles)):
            if n + 1 < len(tiles):
                score(n + 1, *tiles[n + 1][:2], t)
            elif n > 0:
                score(0, *following)
            factor = soften(n)
            if len(tiles) == 1:
                score(0, *following)
            mix(n, factor)

    order = [(dx, dy) for dy in (2, 1, 3, 0) for dx in (1, 0)]

    def each(action, t):
        for dx, dy in order:
            row, local = lax.rem(place_x + dx, 2), lax.rem(place_y + dy, RING)

            @pl.when(local < heads)
            def _():
                action(heads * row + local, t)

    mine = [half_rows(core, t) for t in range(2)]
    theirs = [half_rows(other, t) for t in range(2)]
    far_rows = [
        [pl.ds(pl.multiple_of(core * part + t * tile + n * (tile // 2), 128), tile // 2) for n in range(2)]
        for t in range(2)
    ]

    def piece_of(source, span, piece):
        return gathered.at[source, span, pl.ds(pl.multiple_of(piece * HD, HD), HD)]

    def ring(source, span, piece, target, send, recv):
        return pltpu.make_async_remote_copy(
            src_ref=piece_of(source, span, piece), dst_ref=piece_of(source, span, piece),
            send_sem=send.at[piece], recv_sem=recv.at[piece],
            device_id=(ctx, target * 2 + core), device_id_type=MESH,
        )

    def to_pair(source, piece, t):
        return pltpu.make_async_remote_copy(
            src_ref=piece_of(source, mine[t], piece), dst_ref=piece_of(source, mine[t], piece),
            send_sem=pair_send.at[t, source, piece], recv_sem=pair_sem.at[t, source],
            device_id=sibling, device_id_type=MESH,
        )

    def piece_landed(source, span, piece, sem):
        here = piece_of(source, span, piece)
        pltpu.make_async_copy(here, here, sem.at[piece]).wait()

    def up(piece, t):
        return ring(z, mine[t], piece, z_up, ring_send.at[t, 0], ring_sem.at[t, 0])

    def down(piece, t):
        return ring(z, mine[t], piece, z_down, ring_send.at[t, 1], ring_sem.at[t, 1])

    def relay_up(piece, t):
        return ring(z_down, far_rows[t][0], piece, z_up, relay_send.at[t, 0], relay_sem.at[t, 0])

    def relay_down(piece, t):
        return ring(z_up, far_rows[t][1], piece, z_down, relay_send.at[t, 1], relay_sem.at[t, 1])

    def send_own(piece, t):
        piece_landed(z, mine[t], piece, mixed_sem.at[t])
        up(piece, t).start()
        down(piece, t).start()
        to_pair(z, piece, t).start()

    def pass_on(piece, t):
        piece_landed(z_down, mine[t], piece, ring_sem.at[t, 0])
        relay_up(piece, t).start()
        to_pair(z_down, piece, t).start()
        piece_landed(z_up, mine[t], piece, ring_sem.at[t, 1])
        relay_down(piece, t).start()
        to_pair(z_up, piece, t).start()

    def take_far(piece, t):
        piece_landed(z_far, far_rows[t][0], piece, relay_sem.at[t, 0])
        piece_landed(z_far, far_rows[t][1], piece, relay_sem.at[t, 1])
        to_pair(z_far, piece, t).start()

    @pl.when(works)
    def _():
        def block_at(step):
            dx = jnp.where((step == 3) | (step == 4) | (step == 5) | (step == 7), 1, 0)
            dy = jnp.where(
                (step == 1) | (step == 4), 1, jnp.where((step == 2) | (step == 5), 3, jnp.where(step >= 6, 2, 0))
            )
            return lax.rem(place_x + dx, 2) * RING + lax.rem(place_y + dy, RING)

        def receive(step):
            block = block_at(step)
            span = pl.ds(pl.multiple_of(core * part, 128), part)
            arrived = kv_in.at[block, :, span]
            pltpu.make_async_copy(arrived, arrived, kv_sem.at[block]).wait()
            share(block).start()

        receive(0)

        def limits(shape, dim):
            index = lax.broadcasted_iota(jnp.int32, shape, dim)
            begin, end = jnp.zeros(shape, jnp.int32), jnp.zeros(shape, jnp.int32)
            last = jnp.int32(0)
            for n in range(lengths_ref.shape[0]):
                begin = jnp.where(index == n, last, begin)
                last = last + lengths_ref[n]
                end = jnp.where(index == n, last, end)
            return begin, end

        q_begin, q_end = limits((8, HD), 1)
        k_begin, k_end = limits((8, HD), 0)

        def blank(block, carry):
            start = (half * BLOCKS + block) * rows
            place_q = lax.broadcasted_iota(jnp.int32, (part // 8, 8, HD), 0) * 8
            place_q = place_q + lax.broadcasted_iota(jnp.int32, (part // 8, 8, HD), 1) + (start + core * part)
            same = (place_q >= q_begin[None]) & (place_q < q_end[None])
            lanes_q = jnp.where(same, 0.0, OTHER_DOC).reshape(part, HD)
            q_two[block, :, pl.ds(HD, HD)] = lanes_q.astype(jnp.bfloat16)
            for m in range(chunks):
                place_k = lax.broadcasted_iota(jnp.int32, (8, HD), 1) + (start + m * HD)
                same = (place_k >= k_begin) & (place_k < k_end)
                ones = jnp.where(same, 1.0, 0.0)
                ones = jnp.concatenate([ones, jnp.zeros((HD - 8, HD), jnp.float32)], axis=0)
                keys_across[block, pl.ds(HD, HD), pl.ds(m * HD, HD)] = ones.astype(jnp.bfloat16)
            top[block] = jnp.full((part, HD), FLOOR, jnp.float32)
            accum[block] = jnp.zeros((part, 2 * HD), jnp.float32)
            return carry

        lax.fori_loop(0, BLOCKS, blank, 0)

        ahead = BLOCKS - 2

        def take(turn, carry):
            t, step = turn // BLOCKS, lax.rem(turn, BLOCKS)
            for late, away in zip(range(BLOCKS - 3, BLOCKS), (1, 3, 2)):
                @pl.when(turn == late)
                def _():
                    hand_across(away)

            @pl.when(turn < ahead)
            def _():
                receive(turn + 1)

            @pl.when((turn > ahead) & (turn < BLOCKS))
            def _():
                receive(turn)

            block = jnp.where(t == 0, block_at(step), step)

            @pl.when(t == 0)
            def _():
                pltpu.make_async_copy(q_in.at[block], q_in.at[block], q_sem.at[block]).wait()
                q_two[block, :, pl.ds(0, HD)] = q_in[block]
                shared(block).wait()
                keys_across[block, pl.ds(0, HD)] = kv_in[block, 0].T

            def with_past(before):
                past = jnp.where(t == 0, block_at(before), before)
                return jnp.maximum(block, past), jnp.minimum(block, past), False

            whole = lax.rem(step, 4) == 0
            rest_q, rest_k, _ = with_past(jnp.maximum(step - 1, 0))
            rest_q, rest_k = jnp.where(whole, block, rest_q), jnp.where(whole, block, rest_k)
            turning = turn == BLOCKS - 1
            next_q = jnp.where(turning, 0, jnp.where(t == 1, jnp.minimum(step + 1, BLOCKS - 1), block))
            next_k = jnp.where(turning | ((t == 1) & (step >= 3)), 0, jnp.where(t == 1, step, block))
            next_t = jnp.where(turning, 1, t)

            @pl.when((t == 0) & (step < 4))
            def _():
                score(0, rest_q, rest_k, t)

            @pl.when((t == 0) & (step >= 4))
            def _():
                score(0, *with_past(0)[:2], t)

            def four_at_once(count, inner):
                attend([with_past(4 * count + n) for n in range(4)], t, (rest_q, rest_k, t))
                return inner

            lax.fori_loop(0, step // 4, four_at_once, 0)
            for rest in range(4):
                @pl.when(lax.rem(step, 4) == rest)
                def _():
                    pairs = [with_past(step - 1 - n) for n in range(rest)] + [(block, block, True)]
                    attend(pairs, t, (next_q, next_k, next_t))

            @pl.when(t == 1)
            def _():
                finish(block, 1)

            @pl.when(turn == BLOCKS - 1)
            def _():
                def finish_all(count, inner):
                    finish(block_at(BLOCKS - 1 - count), 0)
                    return inner

                lax.fori_loop(0, BLOCKS, finish_all, 0)

            for when, action in ((BLOCKS + 5, send_own), (BLOCKS + 6, pass_on), (BLOCKS + 7, take_far)):
                @pl.when(turn == when)
                def _():
                    each(action, 0)

            return carry

        lax.fori_loop(0, 2 * BLOCKS, take, 0)

    @pl.when(jnp.logical_not(works))
    def _():
        for away in (1, 3, 2):
            hand_across(away)
        for action in (send_own, pass_on, take_far):
            each(action, 0)

    def half_landed(away, t):
        source = lax.rem(z + away, RING)
        here = gathered.at[source, theirs[t]]
        pltpu.make_async_copy(here, here, pair_sem.at[t, source]).wait()

    def project(aways, t, start, last):
        def some_rows(c, carry):
            span = half_rows(c, t)
            product = None if start else total[pl.ds(pl.multiple_of(c * tile, 128), tile)]
            for away in aways:
                source = lax.rem(z + away, RING)
                term = jnp.dot(
                    gathered[source, span], weights[source].reshape(2 * width, out_cols),
                    preferred_element_type=jnp.float32,
                )
                product = term if product is None else product + term
            if last:
                out_ref[span] = product.astype(jnp.bfloat16)
            else:
                total[pl.ds(pl.multiple_of(c * tile, 128), tile)] = product
            return carry

        lax.fori_loop(0, 2, some_rows, 0)

    each(send_own, 1)
    for away in range(RING):
        half_landed(away, 0)
        weights_here(away)
    project((0, 1, 2, 3), 0, True, True)
    each(pass_on, 1)
    for away in (0, 1, 3):
        half_landed(away, 1)
    project((0, 1, 3), 1, True, False)
    each(take_far, 1)
    half_landed(2, 1)
    project((2,), 1, False, True)

    def all_left(piece, t):
        for copy in (up, down, relay_up, relay_down):
            copy(piece, t).wait_send()
        for source in range(RING):
            to_pair(source, piece, t).wait_send()

    for t in range(2):
        each(all_left, t)
    for away in (2, 1, 3):
        for c in range(2):
            weight_copy(away, c).wait_send()
        weight_across(away).wait_send()
    weight_pair().wait_send()
    for group in sends:
        for _, finish in group:
            finish()

    @pl.when(works)
    def _():
        def left(block, carry):
            share(block).wait_send()

            @pl.when(block != place)
            def _():
                for t in range(2):
                    mixed_copy(block, t).wait_send()
            return carry

        lax.fori_loop(0, BLOCKS, left, 0)


def per_device(query, keys, values, doc_lengths, w_out):
    rows, width = query.shape
    heads = width // HD
    part = rows // 2
    out_cols = w_out.shape[1] // lax.axis_size("head")
    dma = pltpu.SemaphoreType.DMA
    pairs = BLOCKS * (BLOCKS + 1) // 2
    flops = pairs * part * rows * 4 * HD + 2 * rows * w_out.shape[1] * width
    return pl.pallas_call(
        kernel,
        out_shape=jax.ShapeDtypeStruct((rows, out_cols), jnp.bfloat16),
        in_specs=[pl.BlockSpec(memory_space=pltpu.SMEM)] + [pl.BlockSpec(memory_space=pl.ANY)] * 4,
        out_specs=pl.BlockSpec(memory_space=pltpu.VMEM),
        scratch_shapes=[
            pltpu.VMEM((BLOCKS, part, HD), jnp.bfloat16),
            pltpu.VMEM((BLOCKS, 2, rows, HD), jnp.bfloat16),
            pltpu.VMEM((BLOCKS, part, 2 * HD), jnp.bfloat16),
            pltpu.VMEM((BLOCKS, 2 * HD, rows), jnp.bfloat16),
            pltpu.VMEM((BLOCKS, part, HD), jnp.float32),
            pltpu.VMEM((BLOCKS, part, 2 * HD), jnp.float32),
            [pltpu.VMEM((part // 2, rows), jnp.float32)] * 4,
            [pltpu.VMEM((part // 2, rows), jnp.bfloat16)] * 4,
            pltpu.VMEM((BLOCKS, part, HD), jnp.bfloat16),
            pltpu.VMEM((RING, rows, 2 * width), jnp.bfloat16),
            pltpu.VMEM((RING, 2, 2, width // 2, out_cols), jnp.bfloat16),
            pltpu.VMEM((part, out_cols), jnp.float32),
            dma((RING, 2, 3)),
            dma((BLOCKS,)),
            dma((BLOCKS,)),
            dma((BLOCKS,)),
            dma((BLOCKS,)),
            dma((2, BLOCKS)),
            dma((2, 2 * heads)),
            dma((RING, 2)),
            dma((RING, 2)),
            dma((RING,)),
            dma((RING,)),
            dma((2, 2, 2 * heads)),
            dma((2, 2, 2 * heads)),
            dma((2, 2, 2 * heads)),
            dma((2, 2, 2 * heads)),
            dma((2, RING, 2 * heads)),
            dma((2, RING)),
        ],
        compiler_params=pltpu.CompilerParams(
            collective_id=0, has_side_effects=True, vmem_limit_bytes=56 * 1024 * 1024
        ),
        cost_estimate=pl.CostEstimate(
            flops=flops, bytes_accessed=16 * 1024 * 1024, transcendentals=pairs * part * rows
        ),
    )(doc_lengths, query, keys, values, w_out.reshape(2, width // 2, w_out.shape[1]))


def solution(mesh):
    return jax.shard_map(
        per_device,
        mesh=mesh,
        in_specs=(P("ctx", "head"), P("ctx", "head"), P("ctx", "head"), P(), P("head", None)),
        out_specs=P("ctx", "head"),
        check_vma=False,
    )
```

```python
import functools
import math

import jax
import jax.numpy as jnp
from jax import lax
from jax.experimental import pallas as pl
from jax.experimental.pallas import tpu as pltpu
from jax.sharding import PartitionSpec as P

HD = 128
BLOCKS = 8
RING = 4
OTHER_DOC = -(2.0**20)
FLOOR = -5e5
MESH = pl.DeviceIdType.MESH


def kernel(
    lengths_ref, q_ref, k_ref, v_ref, w_ref, out_ref,
    laid, q_in, kv_in, q_two, keys_across, top, accum, scores, shares, mixed, gathered, weights, total,
    laid_sem, send_sem, q_sem, kv_sem, share_send, share_sem, mixed_send, mixed_sem,
    w_send, w_sem, across_send, across_sem, ring_send, ring_sem, relay_send, relay_sem, pair_send, pair_sem,
):
    rows = q_ref.shape[0]
    part = rows // 2
    heads = q_ref.shape[1] // HD
    width = heads * HD
    out_cols = out_ref.shape[1]
    ctx, head = lax.axis_index("ctx"), lax.axis_index("head")
    half, place = ctx // BLOCKS, lax.rem(ctx, BLOCKS)
    place_x, place_y = place // RING, lax.rem(place, RING)
    z, core = head // 2, lax.rem(head, 2)
    other = 1 - core
    first = half * BLOCKS
    sibling = (ctx, z * 2 + other)
    z_up, z_down, z_far = lax.rem(z + 1, RING), lax.rem(z + 3, RING), lax.rem(z + 2, RING)
    works = place_y < heads
    partner = ((RING - 1 - ctx // RING) * RING + place_y, head)

    def lay_out(n, local):
        source = (k_ref, v_ref, q_ref)[n].at[:, pl.ds(local * HD, HD)]
        return pltpu.make_async_copy(source, laid.at[n, local], laid_sem.at[n, local])

    for n in range(3):
        for local in range(heads):
            lay_out(n, local).start()

    barrier = pltpu.get_barrier_semaphore()
    for block in range(BLOCKS):
        for c in range(2):
            @pl.when((block != place) | (c != core))
            def _():
                pl.semaphore_signal(
                    barrier, inc=1, device_id=(first + block, z * 2 + c), device_id_type=MESH
                )
    for away in range(1, RING):
        for c in range(2):
            pl.semaphore_signal(
                barrier, inc=1, device_id=(ctx, lax.rem(z + away, RING) * 2 + c), device_id_type=MESH
            )
    pl.semaphore_signal(barrier, inc=1, device_id=partner, device_id_type=MESH)
    pl.semaphore_wait(barrier, 2 * BLOCKS - 1 + 2 * (RING - 1) + 1)

    def outgoing(away, c, n):
        local = lax.rem(place_y + away, RING)
        target = core * RING + local
        span = pl.ds(c * part, part)
        source = laid.at[n, jnp.minimum(local, heads - 1), span]
        dest, sem = (
            (kv_in.at[place, 0, span], kv_sem.at[place]),
            (kv_in.at[place, 1, span], kv_sem.at[place]),
            (q_in.at[place], q_sem.at[place]),
        )[n]
        here = target == place

        def remote():
            return pltpu.make_async_remote_copy(
                src_ref=source, dst_ref=dest, send_sem=send_sem.at[away, c, n], recv_sem=sem,
                device_id=(first + target, z * 2 + c), device_id_type=MESH,
            )

        def start():
            if away == 0:
                @pl.when((local < heads) & here & (core == c))
                def _():
                    pltpu.make_async_copy(source, dest, sem).start()

                @pl.when((local < heads) & jnp.logical_not(here & (core == c)))
                def _():
                    remote().start()
            else:
                @pl.when(local < heads)
                def _():
                    remote().start()

        def finish():
            sent = local < heads
            if away == 0:
                sent &= jnp.logical_not(here & (core == c))

            @pl.when(sent)
            def _():
                remote().wait_send()

        return start, finish

    def weight_cols(target):
        return pl.ds(pl.multiple_of(target * out_cols, 128), out_cols)

    def weight_copy(away, c):
        target = lax.rem(z + away, RING) * 2 + c
        return pltpu.make_async_remote_copy(
            src_ref=w_ref.at[half, :, weight_cols(target)], dst_ref=weights.at[z, core, half],
            send_sem=w_send.at[away, c], recv_sem=w_sem.at[z, core],
            device_id=(ctx, target), device_id_type=MESH,
        )

    def weight_pair():
        return pltpu.make_async_remote_copy(
            src_ref=w_ref.at[:, :, weight_cols(z * 2 + other)], dst_ref=weights.at[z, core],
            send_sem=w_send.at[0, 0], recv_sem=w_sem.at[z, core],
            device_id=sibling, device_id_type=MESH,
        )

    def weight_across(away):
        piece = weights.at[lax.rem(z + away, RING), :, half]
        return pltpu.make_async_remote_copy(
            src_ref=piece, dst_ref=piece, send_sem=across_send.at[away], recv_sem=across_sem.at[away],
            device_id=partner, device_id_type=MESH,
        )

    def hand_across(away):
        source = lax.rem(z + away, RING)
        for c in range(2):
            piece = weights.at[source, c, half]
            pltpu.make_async_copy(piece, piece, w_sem.at[source, c]).wait()
        weight_across(away).start()

    def weights_here(away):
        source = lax.rem(z + away, RING)
        if away == 0:
            for c in range(2):
                piece = weights.at[source, c]
                pltpu.make_async_copy(piece, piece, w_sem.at[source, c]).wait()
        else:
            piece = weights.at[source, :, 1 - half]
            pltpu.make_async_copy(piece, piece, across_sem.at[away]).wait()

    sends = [[outgoing(away, c, n) for away in (1, 3, 2, 0) for c in range(2)] for n in range(3)]
    for n, (group, away) in enumerate(zip(sends, (2, 1, 3))):
        for local in range(heads):
            lay_out(n, local).wait()
        for start, _ in group:
            start()
        for c in range(2):
            weight_copy(away, c).start()
    weight_pair().start()
    pltpu.make_async_copy(w_ref.at[:, :, weight_cols(head)], weights.at[z, core], w_sem.at[z, core]).start()

    scale = math.log2(math.e) / math.sqrt(HD)
    hh = heads * place_x + place_y

    def share(block):
        span = pl.ds(pl.multiple_of(core * part, 128), part)
        return pltpu.make_async_remote_copy(
            src_ref=kv_in.at[block, :, span], dst_ref=kv_in.at[block, :, span],
            send_sem=share_send.at[block], recv_sem=share_sem.at[block],
            device_id=sibling, device_id_type=MESH,
        )

    def shared(block):
        span = pl.ds(pl.multiple_of(other * part, 128), part)
        return pltpu.make_async_copy(
            kv_in.at[block, :, span], kv_in.at[block, :, span], share_sem.at[block]
        )

    tile, group = part // 2, 16
    chunks = rows // HD

    def half_rows(c, t):
        return pl.ds(pl.multiple_of(c * part + t * tile, 128), tile)

    def mixed_target(t):
        return gathered.at[z, half_rows(core, t), pl.ds(pl.multiple_of(hh * HD, HD), HD)]

    def mixed_source(block, t):
        return mixed.at[block, pl.ds(pl.multiple_of(t * tile, 128), tile)]

    def mixed_copy(block, t):
        return pltpu.make_async_remote_copy(
            src_ref=mixed_source(block, t), dst_ref=mixed_target(t),
            send_sem=mixed_send.at[t, block], recv_sem=mixed_sem.at[t, hh],
            device_id=(first + block, head), device_id_type=MESH,
        )

    def finish(block, t):
        result = accum[block, pl.ds(pl.multiple_of(t * tile, 128), tile)]
        mixed[block, pl.ds(pl.multiple_of(t * tile, 128), tile)] = (
            result[:, :HD] / result[:, HD:]
        ).astype(jnp.bfloat16)

        @pl.when(block == place)
        def _():
            pltpu.make_async_copy(mixed_source(block, t), mixed_target(t), mixed_sem.at[t, hh]).start()

        @pl.when(block != place)
        def _():
            mixed_copy(block, t).start()

    def attend(tiles, t):
        first_row = pl.multiple_of(t * tile, 128)

        def score(n):
            q_block, k_block, _ = tiles[n]
            scores[n][...] = jnp.dot(
                q_two[q_block, pl.ds(first_row, tile)], keys_across[k_block], preferred_element_type=jnp.float32
            )

        def soften(n):
            q_block, _, diagonal = tiles[n]
            rows_here = pl.ds(first_row, tile)
            old = top[q_block, rows_here]
            news = []
            for g in range(tile // group):
                piece = scores[n][pl.ds(g * group, group)]
                parts = [piece[:, m * HD : (m + 1) * HD] for m in range(chunks)]
                if diagonal:
                    row = core * part + first_row + g * group
                    row = lax.broadcasted_iota(jnp.int32, (group, HD), 0) + row
                    lanes = lax.broadcasted_iota(jnp.int32, (group, HD), 1)
                    parts = [jnp.where(lanes + m * HD <= row, one, OTHER_DOC) for m, one in enumerate(parts)]
                most = functools.reduce(jnp.maximum, parts)
                new = jnp.maximum(old[g * group : (g + 1) * group], jnp.max(most, axis=1, keepdims=True))
                news.append(new)
                weight = [jnp.exp2((one - new) * scale).astype(jnp.bfloat16) for one in parts]
                shares[n][pl.ds(g * group, group)] = jnp.concatenate(weight, axis=1)
            new = jnp.concatenate(news, axis=0)
            top[q_block, rows_here] = new
            return jnp.exp2((old - new) * scale)

        def mix(n, factor):
            q_block, k_block, _ = tiles[n]
            rows_here = pl.ds(first_row, tile)
            values = kv_in[k_block, 1]
            values = jnp.concatenate([values, jnp.ones_like(values)], axis=1)
            product = jnp.dot(shares[n][...], values, preferred_element_type=jnp.float32)
            factor = jnp.concatenate([factor, factor], axis=1)
            accum[q_block, rows_here] = accum[q_block, rows_here] * factor + product

        score(0)
        for n in range(len(tiles)):
            if n + 1 < len(tiles):
                score(n + 1)
            mix(n, soften(n))

    order = [(dx, dy) for dy in (2, 1, 3, 0) for dx in (1, 0)]

    def each(action, t):
        for dx, dy in order:
            row, local = lax.rem(place_x + dx, 2), lax.rem(place_y + dy, RING)

            @pl.when(local < heads)
            def _():
                action(heads * row + local, t)

    mine = [half_rows(core, t) for t in range(2)]
    theirs = [half_rows(other, t) for t in range(2)]
    far_rows = [
        [pl.ds(pl.multiple_of(core * part + t * tile + n * (tile // 2), 128), tile // 2) for n in range(2)]
        for t in range(2)
    ]

    def piece_of(source, span, piece):
        return gathered.at[source, span, pl.ds(pl.multiple_of(piece * HD, HD), HD)]

    def ring(source, span, piece, target, send, recv):
        return pltpu.make_async_remote_copy(
            src_ref=piece_of(source, span, piece), dst_ref=piece_of(source, span, piece),
            send_sem=send.at[piece], recv_sem=recv.at[piece],
            device_id=(ctx, target * 2 + core), device_id_type=MESH,
        )

    def to_pair(source, piece, t):
        return pltpu.make_async_remote_copy(
            src_ref=piece_of(source, mine[t], piece), dst_ref=piece_of(source, mine[t], piece),
            send_sem=pair_send.at[t, source, piece], recv_sem=pair_sem.at[t, source],
            device_id=sibling, device_id_type=MESH,
        )

    def piece_landed(source, span, piece, sem):
        here = piece_of(source, span, piece)
        pltpu.make_async_copy(here, here, sem.at[piece]).wait()

    def up(piece, t):
        return ring(z, mine[t], piece, z_up, ring_send.at[t, 0], ring_sem.at[t, 0])

    def down(piece, t):
        return ring(z, mine[t], piece, z_down, ring_send.at[t, 1], ring_sem.at[t, 1])

    def relay_up(piece, t):
        return ring(z_down, far_rows[t][0], piece, z_up, relay_send.at[t, 0], relay_sem.at[t, 0])

    def relay_down(piece, t):
        return ring(z_up, far_rows[t][1], piece, z_down, relay_send.at[t, 1], relay_sem.at[t, 1])

    def send_own(piece, t):
        piece_landed(z, mine[t], piece, mixed_sem.at[t])
        up(piece, t).start()
        down(piece, t).start()
        to_pair(z, piece, t).start()

    def pass_on(piece, t):
        piece_landed(z_down, mine[t], piece, ring_sem.at[t, 0])
        relay_up(piece, t).start()
        to_pair(z_down, piece, t).start()
        piece_landed(z_up, mine[t], piece, ring_sem.at[t, 1])
        relay_down(piece, t).start()
        to_pair(z_up, piece, t).start()

    def take_far(piece, t):
        piece_landed(z_far, far_rows[t][0], piece, relay_sem.at[t, 0])
        piece_landed(z_far, far_rows[t][1], piece, relay_sem.at[t, 1])
        to_pair(z_far, piece, t).start()

    @pl.when(works)
    def _():
        def block_at(step):
            dx = jnp.where((step == 3) | (step == 4) | (step == 5) | (step == 7), 1, 0)
            dy = jnp.where(
                (step == 1) | (step == 4), 1, jnp.where((step == 2) | (step == 5), 3, jnp.where(step >= 6, 2, 0))
            )
            return lax.rem(place_x + dx, 2) * RING + lax.rem(place_y + dy, RING)

        def receive(step):
            block = block_at(step)
            span = pl.ds(pl.multiple_of(core * part, 128), part)
            arrived = kv_in.at[block, :, span]
            pltpu.make_async_copy(arrived, arrived, kv_sem.at[block]).wait()
            share(block).start()

        receive(0)

        def limits(shape, dim):
            index = lax.broadcasted_iota(jnp.int32, shape, dim)
            begin, end = jnp.zeros(shape, jnp.int32), jnp.zeros(shape, jnp.int32)
            last = jnp.int32(0)
            for n in range(lengths_ref.shape[0]):
                begin = jnp.where(index == n, last, begin)
                last = last + lengths_ref[n]
                end = jnp.where(index == n, last, end)
            return begin, end

        q_begin, q_end = limits((8, HD), 1)
        k_begin, k_end = limits((8, HD), 0)

        def blank(block, carry):
            start = (half * BLOCKS + block) * rows
            place_q = lax.broadcasted_iota(jnp.int32, (part // 8, 8, HD), 0) * 8
            place_q = place_q + lax.broadcasted_iota(jnp.int32, (part // 8, 8, HD), 1) + (start + core * part)
            same = (place_q >= q_begin[None]) & (place_q < q_end[None])
            lanes_q = jnp.where(same, 0.0, OTHER_DOC).reshape(part, HD)
            q_two[block, :, pl.ds(HD, HD)] = lanes_q.astype(jnp.bfloat16)
            for m in range(chunks):
                place_k = lax.broadcasted_iota(jnp.int32, (8, HD), 1) + (start + m * HD)
                same = (place_k >= k_begin) & (place_k < k_end)
                ones = jnp.where(same, 1.0, 0.0)
                ones = jnp.concatenate([ones, jnp.zeros((HD - 8, HD), jnp.float32)], axis=0)
                keys_across[block, pl.ds(HD, HD), pl.ds(m * HD, HD)] = ones.astype(jnp.bfloat16)
            top[block] = jnp.full((part, HD), FLOOR, jnp.float32)
            accum[block] = jnp.zeros((part, 2 * HD), jnp.float32)
            return carry

        lax.fori_loop(0, BLOCKS, blank, 0)

        ahead = BLOCKS - 2

        def take(turn, carry):
            t, step = turn // BLOCKS, lax.rem(turn, BLOCKS)
            for late, away in ((BLOCKS - 1, 1), (BLOCKS - 1, 3), (BLOCKS - 1, 2)):
                @pl.when(turn == late)
                def _():
                    hand_across(away)

            @pl.when(turn < ahead)
            def _():
                receive(turn + 1)

            @pl.when((turn > ahead) & (turn < BLOCKS))
            def _():
                receive(turn)

            block = jnp.where(t == 0, block_at(step), step)

            @pl.when(t == 0)
            def _():
                pltpu.make_async_copy(q_in.at[block], q_in.at[block], q_sem.at[block]).wait()
                q_two[block, :, pl.ds(0, HD)] = q_in[block]
                shared(block).wait()
                keys_across[block, pl.ds(0, HD)] = kv_in[block, 0].T

            def with_past(before):
                past = jnp.where(t == 0, block_at(before), before)
                return jnp.maximum(block, past), jnp.minimum(block, past), False

            def four_at_once(count, inner):
                attend([with_past(4 * count + n) for n in range(4)], t)
                return inner

            lax.fori_loop(0, step // 4, four_at_once, 0)
            for rest in range(4):
                @pl.when(lax.rem(step, 4) == rest)
                def _():
                    attend([with_past(step - 1 - n) for n in range(rest)] + [(block, block, True)], t)

            @pl.when(t == 1)
            def _():
                finish(block, 1)

            @pl.when(turn == BLOCKS - 1)
            def _():
                def finish_all(count, inner):
                    finish(block_at(BLOCKS - 1 - count), 0)
                    return inner

                lax.fori_loop(0, BLOCKS, finish_all, 0)

            for when, action in ((BLOCKS + 5, send_own), (BLOCKS + 6, pass_on), (BLOCKS + 7, take_far)):
                @pl.when(turn == when)
                def _():
                    each(action, 0)

            return carry

        lax.fori_loop(0, 2 * BLOCKS, take, 0)

    @pl.when(jnp.logical_not(works))
    def _():
        for away in (1, 3, 2):
            hand_across(away)
        for action in (send_own, pass_on, take_far):
            each(action, 0)

    def half_landed(away, t):
        source = lax.rem(z + away, RING)
        here = gathered.at[source, theirs[t]]
        pltpu.make_async_copy(here, here, pair_sem.at[t, source]).wait()

    def project(aways, t, start, last):
        def some_rows(c, carry):
            span = half_rows(c, t)
            product = None if start else total[pl.ds(pl.multiple_of(c * tile, 128), tile)]
            for away in aways:
                source = lax.rem(z + away, RING)
                term = jnp.dot(
                    gathered[source, span], weights[source].reshape(2 * width, out_cols),
                    preferred_element_type=jnp.float32,
                )
                product = term if product is None else product + term
            if last:
                out_ref[span] = product.astype(jnp.bfloat16)
            else:
                total[pl.ds(pl.multiple_of(c * tile, 128), tile)] = product
            return carry

        lax.fori_loop(0, 2, some_rows, 0)

    each(send_own, 1)
    for away in range(RING):
        half_landed(away, 0)
        weights_here(away)
    project((0, 1, 2, 3), 0, True, True)
    each(pass_on, 1)
    for away in (0, 1, 3):
        half_landed(away, 1)
    project((0, 1, 3), 1, True, False)
    each(take_far, 1)
    half_landed(2, 1)
    project((2,), 1, False, True)

    def all_left(piece, t):
        for copy in (up, down, relay_up, relay_down):
            copy(piece, t).wait_send()
        for source in range(RING):
            to_pair(source, piece, t).wait_send()

    for t in range(2):
        each(all_left, t)
    for away in (2, 1, 3):
        for c in range(2):
            weight_copy(away, c).wait_send()
        weight_across(away).wait_send()
    weight_pair().wait_send()
    for group in sends:
        for _, finish in group:
            finish()

    @pl.when(works)
    def _():
        def left(block, carry):
            share(block).wait_send()

            @pl.when(block != place)
            def _():
                for t in range(2):
                    mixed_copy(block, t).wait_send()
            return carry

        lax.fori_loop(0, BLOCKS, left, 0)


def per_device(query, keys, values, doc_lengths, w_out):
    rows, width = query.shape
    heads = width // HD
    part = rows // 2
    out_cols = w_out.shape[1] // lax.axis_size("head")
    dma = pltpu.SemaphoreType.DMA
    pairs = BLOCKS * (BLOCKS + 1) // 2
    flops = pairs * part * rows * 4 * HD + 2 * rows * w_out.shape[1] * width
    return pl.pallas_call(
        kernel,
        out_shape=jax.ShapeDtypeStruct((rows, out_cols), jnp.bfloat16),
        in_specs=[pl.BlockSpec(memory_space=pltpu.SMEM)] + [pl.BlockSpec(memory_space=pl.ANY)] * 4,
        out_specs=pl.BlockSpec(memory_space=pltpu.VMEM),
        scratch_shapes=[
            pltpu.VMEM((3, heads, rows, HD), jnp.bfloat16),
            pltpu.VMEM((BLOCKS, part, HD), jnp.bfloat16),
            pltpu.VMEM((BLOCKS, 2, rows, HD), jnp.bfloat16),
            pltpu.VMEM((BLOCKS, part, 2 * HD), jnp.bfloat16),
            pltpu.VMEM((BLOCKS, 2 * HD, rows), jnp.bfloat16),
            pltpu.VMEM((BLOCKS, part, HD), jnp.float32),
            pltpu.VMEM((BLOCKS, part, 2 * HD), jnp.float32),
            [pltpu.VMEM((part // 2, rows), jnp.float32)] * 4,
            [pltpu.VMEM((part // 2, rows), jnp.bfloat16)] * 4,
            pltpu.VMEM((BLOCKS, part, HD), jnp.bfloat16),
            pltpu.VMEM((RING, rows, 2 * width), jnp.bfloat16),
            pltpu.VMEM((RING, 2, 2, width // 2, out_cols), jnp.bfloat16),
            pltpu.VMEM((part, out_cols), jnp.float32),
            dma((3, heads)),
            dma((RING, 2, 3)),
            dma((BLOCKS,)),
            dma((BLOCKS,)),
            dma((BLOCKS,)),
            dma((BLOCKS,)),
            dma((2, BLOCKS)),
            dma((2, 2 * heads)),
            dma((RING, 2)),
            dma((RING, 2)),
            dma((RING,)),
            dma((RING,)),
            dma((2, 2, 2 * heads)),
            dma((2, 2, 2 * heads)),
            dma((2, 2, 2 * heads)),
            dma((2, 2, 2 * heads)),
            dma((2, RING, 2 * heads)),
            dma((2, RING)),
        ],
        compiler_params=pltpu.CompilerParams(
            collective_id=0, has_side_effects=True, vmem_limit_bytes=56 * 1024 * 1024
        ),
        cost_estimate=pl.CostEstimate(
            flops=flops, bytes_accessed=16 * 1024 * 1024, transcendentals=pairs * part * rows
        ),
    )(doc_lengths, query, keys, values, w_out.reshape(2, width // 2, w_out.shape[1]))


def solution(mesh):
    return jax.shard_map(
        per_device,
        mesh=mesh,
        in_specs=(P("ctx", "head"), P("ctx", "head"), P("ctx", "head"), P(), P("head", None)),
        out_specs=P("ctx", "head"),
        check_vma=False,
    )
```
